512 devices in a mesh: member: 32 (over y, x), region: 16 (over z, core).
Axes of the slice: x: 4, y: 8, z: 8, core: 2. Of those that a mesh axis runs over, the one named last changes fastest.
Arguments:
- background_spread: bfloat16 [256, 512, 6, 128], P('member', 'region'), may hold values from -6 to 6
- sensed_anomalies: bfloat16 [256, 512, 128], P('member', 'region'), may hold values from -6 to 6
- misfit_vector: bfloat16 [512, 128], P('region'), may hold values from -6 to 6
- damped_precision: float32 [512, 4, 128], P('region'), may hold values from 0.05 to 1
- sensed_patch_table: int32 [512, 4], P('region'), may hold values from 0 to 37, as said below
- zone_patch_tally: int32 [16], P('region'), may hold values from 2 to 32, as said below
Outputs:
- analysis: bfloat16 [256, 512, 6, 128], P('member', 'region')
The draws below stay inside these ranges and needn't reach their ends.
Inputs may be any that keep to these rules, and one draw needn't show every extreme that they name: `sensed_patch_table`: for each region the live slots' lists run across the region's observation blocks from the first to the last; the first live slot uses index 0 and the last live slot the largest index. `zone_patch_tally`: some region has all 32 slots live.
All inputs are finite; a program needn't handle non-finite values.
Results may differ from the reference program's by a relative error of at most 0.0034.
Values may be sent and summed in bfloat16 or wider, within the bound.
No kernel may reach another device: no remote copies, remote signals or barrier semaphores. Data moves between devices by JAX's collectives and lax.ppermute only.
A program may use at most 64 MiB of HBM per device.

```python
import math
import jax
import jax.numpy as jnp
from jax import lax

MEMBERSHIP = 256
CELL_FIELDS = 6
PATCH_CELLS = 128
OB = 128
USED_OBS_BLOCKS = 4
HW = 3
NS_STEPS = 5
BPR = 32
OBR = 32
PATCH_SLOTS_ALL = 512
NOBB = 512


def region_counts(key):
    regions = PATCH_SLOTS_ALL // BPR
    counts = jax.random.randint(jax.random.fold_in(key, 11), (regions,), 2, BPR + 1)
    selected = jax.random.randint(jax.random.fold_in(key, 12), (), 0, regions)
    return jnp.where(jnp.arange(regions) == selected, BPR, counts).astype(jnp.int32)


def draw_zone_patch_tally(key, part):
    return region_counts(key)


def draw_sensed_patch_table(key, part):
    counts = region_counts(key)
    key = jax.random.fold_in(key, 5)
    slots = jnp.arange(PATCH_SLOTS_ALL, dtype=jnp.int32)
    region_id = slots // BPR
    inner_number = slots % BPR
    active_count = counts[region_id]
    placed = jnp.minimum(inner_number, active_count - 1)
    centre = HW + placed * (OBR - 1) // (active_count - 1)
    member_deviation = 2 * HW + 1
    start_positions = jnp.arange(member_deviation, dtype=jnp.int32)
    ranking_values = jax.random.randint(key, (PATCH_SLOTS_ALL, member_deviation), 0, 1000) * member_deviation + start_positions[None]
    leading_extra = ((inner_number == 0)[:, None] & (start_positions == 0)[None]).astype(jnp.int32) * 10000000
    trailing_extra = ((inner_number == active_count - 1)[:, None] & (start_positions == member_deviation - 1)[None]).astype(jnp.int32) * 10000000
    selected = jax.lax.top_k(ranking_values + leading_extra + trailing_extra, USED_OBS_BLOCKS)[1].astype(jnp.int32)
    return (centre[:, None] + selected - HW).astype(jnp.int32)


def steps_of(key, extent, cuts, smallest, largest):
    def one(axis_at, blocks):
        steps = jax.random.uniform(jax.random.fold_in(jax.random.fold_in(key, 6), axis_at), (blocks,), jnp.float32, smallest / len(cuts), largest / len(cuts))
        return jnp.repeat(jnp.exp(steps), extent[axis_at] // blocks).reshape((-1,) + (1,) * (len(extent) - axis_at - 1))

    gain = one(*cuts[0])
    for cut in cuts[1:]:
        gain = gain * one(*cut)
    return gain


def bell_draw(key, dims, scale, limit, cuts=(), kind=jnp.bfloat16):
    values = jax.random.normal(key, dims, jnp.float32) * scale
    if len(cuts) > 0:
        values = steps_of(key, dims, cuts, -0.22, 0.18) * values
    return jnp.clip(values, min=-limit, max=limit).astype(kind)


def setup_inputs(seed: int = 0) -> dict:
    seeds = jax.random.split(jax.random.key(seed), 7)
    return {
        "background_spread": bell_draw(seeds[0], (MEMBERSHIP, PATCH_SLOTS_ALL, CELL_FIELDS, PATCH_CELLS), 1.0, 6.0, ((0, 32), (1, 16))),
        "sensed_anomalies": bell_draw(seeds[1], (MEMBERSHIP, NOBB, OB), 1.0, 6.0, ((0, 32), (1, 16))),
        "misfit_vector": bell_draw(seeds[2], (NOBB, OB), 1.0, 6.0, ((0, 16),)),
        "damped_precision": jnp.clip(jnp.exp(math.log(1.0) - 2.9957323 * jax.random.uniform(seeds[3], (PATCH_SLOTS_ALL, USED_OBS_BLOCKS, OB), jnp.float32) ** steps_of(seeds[3], (PATCH_SLOTS_ALL, USED_OBS_BLOCKS, OB), ((0, 16),), -0.2, 0.2)), 0.05, 1.0),
        "sensed_patch_table": draw_sensed_patch_table(jax.random.fold_in(seeds[6], 71), 0),
        "zone_patch_tally": draw_zone_patch_tally(jax.random.fold_in(seeds[6], 71), 0),
    }


def matmul_high(left, right):
    return jnp.einsum('bkj,bjl->bkl', left, right, precision=lax.Precision.HIGHEST)

def analyse(background_field, yb, loc, innov):
    sample_lines = background_field.shape[0]
    scaled = (yb.astype(jnp.float32) * loc[None]).astype(jnp.bfloat16)
    gram = jnp.einsum('kbp,jbp->bkj', scaled, yb, preferred_element_type=jnp.float32)
    drive = jnp.einsum('kbp,bp->bk', scaled, innov, preferred_element_type=jnp.float32)
    ident = jnp.eye(sample_lines, dtype=jnp.float32)[None]
    amat = ident + gram / jnp.float32(sample_lines - 1)
    frob = jnp.sqrt(lax.optimization_barrier(jnp.sum(amat * amat, axis=(1, 2))))[:, None, None]
    upper = amat / frob
    lower = jnp.broadcast_to(ident, amat.shape)
    for step in range(NS_STEPS):
        middle = 1.5 * ident - 0.5 * matmul_high(lower, upper)
        upper = matmul_high(upper, middle)
        lower = matmul_high(middle, lower)
    trans = lower / jnp.sqrt(frob)
    inner = jnp.einsum('bkj,bj->bk', trans, drive, precision=lax.Precision.HIGHEST)
    wmean = jnp.einsum('bkj,bj->bk', trans, inner, precision=lax.Precision.HIGHEST) / jnp.float32(sample_lines - 1)
    weights = (trans + wmean[:, :, None]).astype(jnp.bfloat16)
    mean_state = lax.optimization_barrier(jnp.mean(background_field.astype(jnp.float32), axis=0))
    mixed = jnp.einsum('kbc,bkj->jbc', background_field, weights, preferred_element_type=jnp.float32)
    colsum = lax.optimization_barrier(jnp.sum(weights.astype(jnp.float32), axis=1))
    return mean_state[None] + mixed - mean_state[None] * jnp.transpose(colsum)[:, :, None]

def reference(background_spread, sensed_anomalies, misfit_vector, damped_precision, sensed_patch_table, zone_patch_tally):
    sample_lines = background_spread.shape[0]
    stretch_breadth = background_spread.shape[2] * background_spread.shape[3]

    def one_slot(patch_place):
        region_id = patch_place // BPR
        inner_number = patch_place % BPR
        blocks = (region_id * OBR - HW + sensed_patch_table[patch_place]) % NOBB
        blocks = blocks.astype(jnp.int32)
        yb = jnp.take(sensed_anomalies, blocks, axis=1).reshape(sample_lines, 1, USED_OBS_BLOCKS * OB)
        innov = jnp.take(misfit_vector, blocks, axis=0).reshape(1, USED_OBS_BLOCKS * OB)
        loc = damped_precision[patch_place].reshape(1, USED_OBS_BLOCKS * OB)
        background_field = lax.dynamic_index_in_dim(background_spread, patch_place, 1, keepdims=False).reshape(sample_lines, 1, stretch_breadth)

        def solve_slot(unused):
            return analyse(background_field, yb, loc, innov).astype(jnp.bfloat16)

        def keep_slot(unused):
            return background_field
        live = inner_number < zone_patch_tally[region_id]
        return lax.cond(live, solve_slot, keep_slot, 0)[:, 0]
    updated_result = lax.map(one_slot, jnp.arange(PATCH_SLOTS_ALL, dtype=jnp.int32))
    return jnp.transpose(updated_result, (1, 0, 2)).reshape(background_spread.shape)
```

```python
import jax
import jax.numpy as jnp
from jax import lax
from jax.sharding import PartitionSpec as P

HW = 3
NS_STEPS = 5


def with_halo(cells, axis, dim, width):
    count = lax.axis_size(axis)
    head = lax.slice_in_dim(cells, 0, width, axis=dim)
    tail = lax.slice_in_dim(cells, cells.shape[dim] - width, cells.shape[dim], axis=dim)
    return jnp.concatenate(
        [
            lax.ppermute(tail, axis, [(i, (i + 1) % count) for i in range(count)]),
            cells,
            lax.ppermute(head, axis, [((i + 1) % count, i) for i in range(count)]),
        ],
        axis=dim,
    )


def matmul_high(left, right):
    return jnp.dot(left, right, precision=lax.Precision.HIGHEST)


def analyse(field, yb, loc, innov):
    lines = field.shape[0]
    scaled = (yb.astype(jnp.float32) * loc[None]).astype(jnp.bfloat16)
    gram = jnp.einsum("kp,jp->kj", scaled, yb, preferred_element_type=jnp.float32)
    drive = jnp.einsum("kp,p->k", scaled, innov, preferred_element_type=jnp.float32)
    ident = jnp.eye(lines, dtype=jnp.float32)
    amat = ident + gram / jnp.float32(lines - 1)
    frob = jnp.sqrt(jnp.sum(amat * amat))
    upper = amat / frob
    lower = ident
    for step in range(NS_STEPS):
        if step == 0:
            middle = 1.5 * ident - 0.5 * upper
            lower = middle
        else:
            middle = 1.5 * ident - 0.5 * matmul_high(lower, upper)
            lower = matmul_high(middle, lower)
        if step + 1 < NS_STEPS:
            upper = matmul_high(upper, middle)
    trans = lower / jnp.sqrt(frob)
    inner = jnp.dot(trans, drive, precision=lax.Precision.HIGHEST)
    wmean = jnp.dot(trans, inner, precision=lax.Precision.HIGHEST) / jnp.float32(lines - 1)
    weights = (trans + wmean[:, None]).astype(jnp.bfloat16)
    mean_state = jnp.mean(field.astype(jnp.float32), axis=0)
    mixed = jnp.einsum("kc,kj->jc", field, weights, preferred_element_type=jnp.float32)
    colsum = jnp.sum(weights.astype(jnp.float32), axis=0)
    return mean_state[None] + mixed - mean_state[None] * colsum[:, None]


def one_hot_rows(indices, extent):
    return (indices.reshape(-1)[:, None] == jnp.arange(extent, dtype=jnp.int32)[None]).astype(
        jnp.bfloat16
    )


def shards(forecast, anomalies, misfit, precision, table, tally):
    members, slots, fields, cells = forecast.shape
    used = table.shape[1]
    obs = anomalies.shape[2]
    ranks = lax.axis_size("member")
    stacked = jnp.concatenate([anomalies, misfit[None]], axis=0)
    extended = with_halo(stacked, "region", 1, HW)
    extent = extended.shape[1]
    me = lax.axis_index("member")
    pick = one_hot_rows(table, extent)
    chosen = jnp.einsum(
        "qe,meo->qmo", pick, extended[:members], preferred_element_type=jnp.float32
    ).astype(jnp.bfloat16)
    chosen = chosen.reshape(slots, used, members, obs)
    outgoing = jnp.concatenate([jnp.transpose(forecast, (1, 2, 0, 3)), chosen], axis=1)
    incoming = lax.all_to_all(outgoing, "member", 0, 0, tiled=True)
    lines = ranks * members
    mine = jnp.transpose(incoming, (0, 2, 1, 3)).reshape(lines, -1)
    field = mine[:, : fields * cells]
    yb = mine[:, fields * cells :]
    pick_mine = lax.dynamic_slice_in_dim(pick, me * used, used, 0)
    innov = jnp.dot(pick_mine, extended[members], preferred_element_type=jnp.float32).astype(
        jnp.bfloat16
    )
    innov = innov.reshape(used * obs)
    loc = lax.dynamic_slice_in_dim(precision, me, 1, 0).reshape(used * obs)
    solved = analyse(field, yb, loc, innov).astype(jnp.bfloat16)
    result = jnp.where(me < tally[0], solved, field)
    back = jnp.transpose(result.reshape(ranks, members, fields, cells), (0, 2, 1, 3))
    back = lax.all_to_all(back, "member", 0, 0, tiled=True)
    return jnp.transpose(back, (2, 0, 1, 3))


def solution(mesh):
    return jax.shard_map(
        shards,
        mesh=mesh,
        in_specs=(
            P("member", "region", None, None),
            P("member", "region", None),
            P("region", None),
            P("region", None, None),
            P("region", None),
            P("region"),
        ),
        out_specs=P("member", "region", None, None),
        check_vma=False,
    )
```

```python
import functools
import jax
import jax.numpy as jnp
from jax import lax
from jax.experimental import pallas as pl
from jax.experimental.pallas import tpu as pltpu
from jax.sharding import PartitionSpec as P

HW = 3
NS_STEPS = 5


def with_halo(cells, axis, dim, width):
    count = lax.axis_size(axis)
    head = lax.slice_in_dim(cells, 0, width, axis=dim)
    tail = lax.slice_in_dim(cells, cells.shape[dim] - width, cells.shape[dim], axis=dim)
    return jnp.concatenate(
        [
            lax.ppermute(tail, axis, [(i, (i + 1) % count) for i in range(count)]),
            cells,
            lax.ppermute(head, axis, [((i + 1) % count, i) for i in range(count)]),
        ],
        axis=dim,
    )


def halves(x):
    high = x.astype(jnp.bfloat16)
    return high, (x - high.astype(jnp.float32)).astype(jnp.bfloat16)


def dot(left, right, dims=((1,), (0,))):
    return lax.dot_general(left, right, (dims, ((), ())), preferred_element_type=jnp.float32)


def product(left, right):
    return dot(left[0], right[0]) + (dot(left[0], right[1]) + dot(left[1], right[0]))


def analyse_kernel(fields, live_ref, incoming_ref, loc_ref, innov_ref, out_ref):
    ranks, blocks, members, obs = incoming_ref.shape
    lines = ranks * members

    def rows(block):
        return incoming_ref[:, block].astype(jnp.float32).reshape(lines, obs)

    yb = jnp.concatenate([rows(block) for block in range(fields, blocks)], axis=1)
    scaled = (yb * loc_ref[...]).astype(jnp.bfloat16)
    left = jnp.concatenate([yb, jnp.broadcast_to(innov_ref[...], (16, yb.shape[1]))], axis=0)
    both = dot(left.astype(jnp.bfloat16), scaled, ((1,), (1,)))
    drive = both[lines : lines + 8]
    row = lax.broadcasted_iota(jnp.int32, (lines, lines), 0)
    column = lax.broadcasted_iota(jnp.int32, (lines, lines), 1)
    ident = (row == column).astype(jnp.float32)
    amat = ident + both[:lines] / jnp.float32(lines - 1)
    parts = halves(amat)
    square = product(parts, parts)
    total = jnp.sum(jnp.sum(amat * amat, axis=0, keepdims=True), axis=1, keepdims=True)
    frob = jnp.sqrt(total)
    inverse = 1.0 / frob
    joint = amat * inverse
    lower = 1.5 * ident - 0.5 * joint
    half = 1.5 * joint - (0.5 * inverse * inverse) * square
    joint = 1.5 * half - (0.5 * inverse) * product(halves(half), parts)
    for step in range(1, NS_STEPS):
        parts = halves(joint)
        if step + 1 < NS_STEPS:
            low = halves(lower)
            pair = tuple(jnp.concatenate([j, z], axis=0) for j, z in zip(parts, low))
            pair = product(pair, parts)
            half = 1.5 * joint - 0.5 * pair[:lines]
            lower = 1.5 * lower - 0.5 * pair[lines:]
            joint = 1.5 * half - 0.5 * product(halves(half), parts)
        else:
            lower = 1.5 * lower - 0.5 * product(halves(lower), parts)
    trans = lower * (1.0 / jnp.sqrt(frob))
    parts = halves(trans)
    inner = product(halves(drive), parts)
    wmean = product(halves(inner), parts) / jnp.float32(lines - 1)
    weights = (trans + wmean[:1]).astype(jnp.bfloat16)
    colsum = jnp.sum(weights.astype(jnp.float32), axis=1, keepdims=True)
    live = live_ref[0] > 0
    for pair in range(0, fields, 2):
        field = jnp.concatenate([rows(pair), rows(pair + 1)], axis=1)
        mean = jnp.sum(field, axis=0, keepdims=True) / jnp.float32(lines)
        mixed = dot(weights, field.astype(jnp.bfloat16)) + mean * (1.0 - colsum)
        mixed = jnp.where(live, mixed, field)
        for i in range(2):
            part = mixed[:, i * obs : (i + 1) * obs].reshape(ranks, members, obs)
            out_ref[:, pair + i] = part.astype(jnp.bfloat16)


def analyse(incoming, fields, loc, innov, live):
    ranks, blocks, members, obs = incoming.shape
    vmem = pl.BlockSpec(memory_space=pltpu.VMEM)
    return pl.pallas_call(
        functools.partial(analyse_kernel, fields),
        out_shape=jax.ShapeDtypeStruct((ranks, fields, members, obs), jnp.bfloat16),
        in_specs=[pl.BlockSpec(memory_space=pltpu.SMEM), vmem, vmem, vmem],
        out_specs=vmem,
        compiler_params=pltpu.CompilerParams(vmem_limit_bytes=32 * 2**20),
        name="analyse",
    )(live, incoming, loc, innov)


def one_hot_rows(indices, extent):
    return (indices.reshape(-1)[:, None] == jnp.arange(extent, dtype=jnp.int32)[None]).astype(
        jnp.bfloat16
    )


def shards(forecast, anomalies, misfit, precision, table, tally):
    members, slots, fields, cells = forecast.shape
    used = table.shape[1]
    obs = anomalies.shape[2]
    ranks = lax.axis_size("member")
    stacked = jnp.concatenate([anomalies, misfit[None]], axis=0)
    extended = with_halo(stacked, "region", 1, HW)
    extent = extended.shape[1]
    me = lax.axis_index("member")
    pick = one_hot_rows(table, extent)
    chosen = jnp.einsum(
        "qe,meo->qmo", pick, extended[:members], preferred_element_type=jnp.float32
    ).astype(jnp.bfloat16)
    chosen = chosen.reshape(slots, used, members, obs)
    outgoing = jnp.concatenate([jnp.transpose(forecast, (1, 2, 0, 3)), chosen], axis=1)
    incoming = lax.all_to_all(outgoing, "member", 0, 0, tiled=True)
    pick_mine = lax.dynamic_slice_in_dim(pick, me * used, used, 0)
    innov = jnp.dot(pick_mine, extended[members], preferred_element_type=jnp.float32).astype(
        jnp.bfloat16
    )
    innov = innov.reshape(1, used * obs).astype(jnp.float32)
    loc = lax.dynamic_slice_in_dim(precision, me, 1, 0).reshape(1, used * obs)
    live = (me < tally).astype(jnp.int32)
    back = analyse(incoming, fields, loc, innov, live)
    back = lax.all_to_all(back, "member", 0, 0, tiled=True)
    return jnp.transpose(back, (2, 0, 1, 3))


def solution(mesh):
    return jax.shard_map(
        shards,
        mesh=mesh,
        in_specs=(
            P("member", "region", None, None),
            P("member", "region", None),
            P("region", None),
            P("region", None, None),
            P("region", None),
            P("region"),
        ),
        out_specs=P("member", "region", None, None),
        check_vma=False,
    )
```

```python
import functools
import jax
import jax.numpy as jnp
from jax import lax
from jax.experimental import pallas as pl
from jax.experimental.pallas import tpu as pltpu
from jax.sharding import PartitionSpec as P

HW = 3
NS_STEPS = 5
VMEM = pl.BlockSpec(memory_space=pltpu.VMEM)
SMEM = pl.BlockSpec(memory_space=pltpu.SMEM)
PARAMS = pltpu.CompilerParams(vmem_limit_bytes=32 * 2**20)


def split(x):
    high = x.astype(jnp.bfloat16)
    return high, (x - high.astype(jnp.float32)).astype(jnp.bfloat16)


def halves(x):
    return jnp.concatenate(split(x), axis=0)


def dot(left, right, dims=((1,), (0,))):
    return lax.dot_general(left, right, (dims, ((), ())), preferred_element_type=jnp.float32)


def narrow(left, right):
    return dot(left.astype(jnp.bfloat16), right.astype(jnp.bfloat16))


def analyse_kernel(
    fields, me_ref, tally_ref, table_ref, incoming_ref, loc_ref, misfit_ref, before_ref, after_ref, out_ref, line_ref
):
    ranks, blocks, members, obs = incoming_ref.shape
    lines = ranks * members
    count = misfit_ref.shape[0]
    me = me_ref[0]

    def rows(block):
        return incoming_ref[:, block].astype(jnp.float32).reshape(lines, obs)

    def across(x):
        return jnp.sum(jnp.sum(x, axis=0, keepdims=True), axis=1, keepdims=True)

    line_ref[HW : HW + count] = misfit_ref[...].astype(jnp.float32)
    for i in range(HW):
        line_ref[i : i + 1] = before_ref[members, i : i + 1].astype(jnp.float32)
        line_ref[HW + count + i : HW + count + i + 1] = after_ref[members, i : i + 1].astype(jnp.float32)
    innov = jnp.concatenate([line_ref[pl.ds(table_ref[h, me], 1)] for h in range(blocks - fields)], axis=1)
    loc = loc_ref[me]
    loc = jnp.concatenate([loc[h : h + 1] for h in range(blocks - fields)], axis=1)
    yb = jnp.concatenate([rows(block) for block in range(fields, blocks)], axis=1)
    scaled = (yb * loc).astype(jnp.bfloat16)
    left = jnp.concatenate([yb, jnp.broadcast_to(innov, (16, yb.shape[1]))], axis=0)
    both = dot(left.astype(jnp.bfloat16), scaled, ((1,), (1,)))
    drive = both[lines : lines + 8]
    row = lax.broadcasted_iota(jnp.int32, (lines, lines), 0)
    column = lax.broadcasted_iota(jnp.int32, (lines, lines), 1)
    ident = (row == column).astype(jnp.float32)
    gram = both[:lines] * (1.0 / (lines - 1))
    amat = gram + ident
    thin, low = split(gram)
    pair = halves(drive)
    square = dot(jnp.concatenate([thin, pair], axis=0), thin)
    tail = square[lines:] + dot(pair, low)
    inverse = lax.rsqrt(across(amat * amat))
    root = jnp.sqrt(inverse)
    centre = across(amat * ident) * (1.0 / lines)

    w, n = inverse, gram * inverse
    t = 1.5 * w - 0.5 * w * w
    h = (1.5 - w) * n - (0.5 * inverse * inverse) * square[:lines]
    vector = (1.5 - 0.5 * w) * drive - (0.5 * inverse) * (tail[:8] + tail[8:])
    n = (1.5 - 0.5 * w) * h - (0.5 * t) * n - 0.5 * narrow(h, n)
    w = 1.5 * t - 0.5 * t * w
    mean = centre * inverse
    z = 1.5 - 0.5 * mean
    r = (-0.5 * inverse) * (gram - (centre - 1.0) * ident)
    mean = mean * z * z
    n = n - (mean - w) * ident
    w = mean
    for step in range(1, NS_STEPS):
        thin, low = split(n)
        last = step + 1 == NS_STEPS
        left = [r.astype(jnp.bfloat16), halves(vector)]
        both = dot(jnp.concatenate(left if last else [thin] + left, axis=0), thin)
        slope = 1.5 - 0.5 * w
        tail = both[both.shape[0] - 16 :] + dot(left[1], low)
        vector = slope * vector - 0.5 * (tail[:8] + tail[8:])
        r = slope * r - (0.5 * z) * n - 0.5 * both[both.shape[0] - 16 - lines : both.shape[0] - 16]
        z = z * slope
        if not last:
            t = slope * w
            h = (1.5 - w) * n - 0.5 * both[:lines]
            n = slope * h - (0.5 * t) * n - 0.5 * dot(h.astype(jnp.bfloat16), thin)
            w = slope * t
    high, low = split(r)
    tail = dot(halves(vector), high) + dot(halves(vector), low)
    wmean = (z * vector + (tail[:8] + tail[8:])) * (root * root * (1.0 / (lines - 1)))
    trans = (r + z * ident) * root
    weights = (trans + wmean[:1]).astype(jnp.bfloat16)
    colsum = jnp.sum(weights.astype(jnp.float32), axis=1, keepdims=True)
    live = me < tally_ref[0]
    for pair in range(0, fields, 2):
        field = jnp.concatenate([rows(pair), rows(pair + 1)], axis=1)
        mean = jnp.sum(field, axis=0, keepdims=True) * (1.0 / lines)
        mixed = dot(weights, field.astype(jnp.bfloat16)) + mean * (1.0 - colsum)
        mixed = jnp.where(live, mixed, field)
        for i in range(2):
            part = mixed[:, i * obs : (i + 1) * obs].reshape(ranks, members, obs)
            out_ref[:, pair + i] = part.astype(jnp.bfloat16)


def pack_kernel(table_ref, forecast_ref, anomalies_ref, out_ref, blocks_ref, held_ref, sems):
    fields = forecast_ref.shape[1]
    copies = [
        pltpu.make_async_copy(forecast_ref.at[:, field], held_ref.at[field], sems.at[field])
        for field in range(fields)
    ]
    for copy in copies:
        copy.start()
    blocks_ref[...] = jnp.swapaxes(anomalies_ref[...], 0, 1)
    for field in range(fields):
        copies[field].wait()
        out_ref[:, field] = jnp.swapaxes(held_ref[field], 0, 1)


def choose_kernel(fields, table_ref, packed_ref, blocks_ref, before_ref, after_ref, out_ref, all_ref):
    count, members, _ = blocks_ref.shape
    all_ref[HW : HW + count] = blocks_ref[...]
    all_ref[:HW] = jnp.swapaxes(before_ref[:members], 0, 1)
    all_ref[HW + count :] = jnp.swapaxes(after_ref[:members], 0, 1)
    out_ref[:, :fields] = packed_ref[...]
    used, slots = table_ref.shape
    for slot in range(slots):
        for h in range(used):
            out_ref[slot, fields + h] = all_ref[table_ref[h, slot]]


def shards(forecast, anomalies, misfit, precision, table, tally):
    members, slots, fields, cells = forecast.shape
    used = table.shape[1]
    count, obs = misfit.shape
    table = jnp.transpose(table)
    ranks = lax.axis_size("member")
    regions = lax.axis_size("region")
    stacked = jnp.concatenate([anomalies, misfit[None]], axis=0)
    up = [(i, (i + 1) % regions) for i in range(regions)]
    before = lax.ppermute(stacked[:, count - HW :], "region", up)
    after = lax.ppermute(stacked[:, :HW], "region", [(j, i) for i, j in up])
    packed, blocks = pl.pallas_call(
        pack_kernel,
        out_shape=(
            jax.ShapeDtypeStruct((slots, fields, members, cells), forecast.dtype),
            jax.ShapeDtypeStruct((count, members, obs), anomalies.dtype),
        ),
        in_specs=[VMEM, pl.BlockSpec(memory_space=pl.ANY), VMEM],
        out_specs=(VMEM, VMEM),
        scratch_shapes=[
            pltpu.VMEM((fields, members, slots, cells), forecast.dtype),
            pltpu.SemaphoreType.DMA((fields,)),
        ],
        compiler_params=PARAMS,
        name="pack",
    )(table, jnp.transpose(forecast, (0, 2, 1, 3)), anomalies)
    outgoing = pl.pallas_call(
        functools.partial(choose_kernel, fields),
        out_shape=jax.ShapeDtypeStruct((slots, fields + used, members, cells), packed.dtype),
        in_specs=[SMEM, VMEM, VMEM, VMEM, VMEM],
        out_specs=VMEM,
        scratch_shapes=[pltpu.VMEM((count + 2 * HW, members, obs), blocks.dtype)],
        compiler_params=PARAMS,
        name="choose",
    )(table, packed, blocks, before, after)
    incoming = lax.all_to_all(outgoing, "member", 0, 0, tiled=True)
    me = lax.axis_index("member").reshape(1)
    back = pl.pallas_call(
        functools.partial(analyse_kernel, fields),
        out_shape=jax.ShapeDtypeStruct((ranks, fields, members, cells), forecast.dtype),
        in_specs=[SMEM, SMEM, SMEM, VMEM, VMEM, VMEM, VMEM, VMEM],
        out_specs=VMEM,
        scratch_shapes=[pltpu.VMEM((count + 2 * HW, obs), jnp.float32)],
        compiler_params=PARAMS,
        name="analyse",
    )(me, tally, table, incoming, precision, misfit, before, after)
    back = lax.all_to_all(back, "member", 0, 0, tiled=True)
    return jnp.transpose(back, (2, 0, 1, 3))


def solution(mesh):
    return jax.shard_map(
        shards,
        mesh=mesh,
        in_specs=(
            P("member", "region", None, None),
            P("member", "region", None),
            P("region", None),
            P("region", None, None),
            P("region", None),
            P("region"),
        ),
        out_specs=P("member", "region", None, None),
        check_vma=False,
    )
```

```python
import functools
import jax
import jax.numpy as jnp
from jax import lax
from jax.experimental import pallas as pl
from jax.experimental.pallas import tpu as pltpu
from jax.sharding import PartitionSpec as P

HW = 3
NS_STEPS = 5
VMEM = pl.BlockSpec(memory_space=pltpu.VMEM)
SMEM = pl.BlockSpec(memory_space=pltpu.SMEM)
PARAMS = pltpu.CompilerParams(vmem_limit_bytes=32 * 2**20)


def split(x):
    high = x.astype(jnp.bfloat16)
    return high, (x - high.astype(jnp.float32)).astype(jnp.bfloat16)


def halves(x):
    return jnp.concatenate(split(x), axis=0)


def dot(left, right, dims=((1,), (0,))):
    return lax.dot_general(left, right, (dims, ((), ())), preferred_element_type=jnp.float32)


def narrow(left, right):
    return dot(left.astype(jnp.bfloat16), right.astype(jnp.bfloat16))


def analyse_kernel(fields, incoming_ref, side_ref, out_ref):
    ranks, blocks, members, obs = incoming_ref.shape
    lines = ranks * members

    def rows(block):
        return incoming_ref[:, block].astype(jnp.float32).reshape(lines, obs)

    def across(x):
        return jnp.sum(jnp.sum(x, axis=0, keepdims=True), axis=1, keepdims=True)

    loc, innov, live = side_ref[0:1], side_ref[1:2], side_ref[2:3, : 2 * obs] > 0
    yb = jnp.concatenate([rows(block) for block in range(fields, blocks)], axis=1)
    scaled = (yb * loc).astype(jnp.bfloat16)
    left = jnp.concatenate([yb, jnp.broadcast_to(innov, (16, yb.shape[1]))], axis=0)
    both = dot(left.astype(jnp.bfloat16), scaled, ((1,), (1,)))
    drive = both[lines : lines + 8]
    row = lax.broadcasted_iota(jnp.int32, (lines, lines), 0)
    column = lax.broadcasted_iota(jnp.int32, (lines, lines), 1)
    ident = (row == column).astype(jnp.float32)
    gram = both[:lines] * (1.0 / (lines - 1))
    amat = gram + ident
    thin, low = split(gram)
    pair = halves(drive)
    square = dot(jnp.concatenate([thin, pair], axis=0), thin)
    tail = square[lines:] + dot(pair, low)
    inverse = lax.rsqrt(across(amat * amat))
    root = jnp.sqrt(inverse)
    centre = across(amat * ident) * (1.0 / lines)

    w, n = inverse, gram * inverse
    t = 1.5 * w - 0.5 * w * w
    h = (1.5 - w) * n - (0.5 * inverse * inverse) * square[:lines]
    vector = (1.5 - 0.5 * w) * drive - (0.5 * inverse) * (tail[:8] + tail[8:])
    n = (1.5 - 0.5 * w) * h - (0.5 * t) * n - 0.5 * narrow(h, n)
    w = 1.5 * t - 0.5 * t * w
    mean = centre * inverse
    z = 1.5 - 0.5 * mean
    r = (-0.5 * inverse) * (gram - (centre - 1.0) * ident)
    mean = mean * z * z
    n = n - (mean - w) * ident
    w = mean
    for step in range(1, NS_STEPS):
        thin, low = split(n)
        last = step + 1 == NS_STEPS
        left = [r.astype(jnp.bfloat16), halves(vector)]
        both = dot(jnp.concatenate(left if last else [thin] + left, axis=0), thin)
        slope = 1.5 - 0.5 * w
        tail = both[both.shape[0] - 16 :] + dot(left[1], low)
        vector = slope * vector - 0.5 * (tail[:8] + tail[8:])
        r = slope * r - (0.5 * z) * n - 0.5 * both[both.shape[0] - 16 - lines : both.shape[0] - 16]
        z = z * slope
        if not last:
            t = slope * w
            h = (1.5 - w) * n - 0.5 * both[:lines]
            n = slope * h - (0.5 * t) * n - 0.5 * dot(h.astype(jnp.bfloat16), thin)
            w = slope * t
    high, low = split(r)
    tail = dot(halves(vector), high) + dot(halves(vector), low)
    wmean = (z * vector + (tail[:8] + tail[8:])) * (root * root * (1.0 / (lines - 1)))
    trans = (r + z * ident) * root
    weights = (trans + wmean[:1]).astype(jnp.bfloat16)
    colsum = jnp.sum(weights.astype(jnp.float32), axis=1, keepdims=True)
    for pair in range(0, fields, 2):
        field = jnp.concatenate([rows(pair), rows(pair + 1)], axis=1)
        mean = jnp.sum(field, axis=0, keepdims=True) * (1.0 / lines)
        mixed = dot(weights, field.astype(jnp.bfloat16)) + mean * (1.0 - colsum)
        mixed = jnp.where(live, mixed, field)
        for i in range(2):
            part = mixed[:, i * obs : (i + 1) * obs].reshape(ranks, members, obs)
            out_ref[:, pair + i] = part.astype(jnp.bfloat16)


def edges_kernel(tail_ref, head_ref, tail_out_ref, head_out_ref):
    tail_out_ref[...] = tail_ref[...]
    head_out_ref[...] = head_ref[...]


def pack_kernel(table_ref, loc_ref, misfit_ref, forecast_ref, anomalies_ref, out_ref, blocks_ref):
    for field in range(forecast_ref.shape[1]):
        out_ref[:, field] = jnp.swapaxes(forecast_ref[:, field], 0, 1)
    blocks_ref[...] = jnp.swapaxes(anomalies_ref[...], 0, 1)


def choose_kernel(
    fields, place_ref, table_ref, packed_ref, blocks_ref, loc_ref, misfit_ref, before_ref, after_ref,
    out_ref, side_ref, all_ref, line_ref
):
    count, members, obs = blocks_ref.shape
    all_ref[HW : HW + count] = blocks_ref[...]
    all_ref[:HW] = jnp.swapaxes(before_ref[:members], 0, 1)
    all_ref[HW + count :] = jnp.swapaxes(after_ref[:members], 0, 1)
    out_ref[:, :fields] = packed_ref[...]
    used, slots = table_ref.shape
    for slot in range(slots):
        for h in range(used):
            out_ref[slot, fields + h] = all_ref[table_ref[h, slot]]
    dead = place_ref[0] >= slots
    me = jnp.where(dead, place_ref[0] - slots, place_ref[0])
    line_ref[HW : HW + count] = misfit_ref[...].astype(jnp.float32)
    line_ref[:HW] = before_ref[members].astype(jnp.float32)
    line_ref[HW + count :] = after_ref[members].astype(jnp.float32)
    loc = loc_ref[me]
    side_ref[...] = jnp.full(side_ref.shape, jnp.where(dead, 0.0, 1.0), jnp.float32)
    for h in range(used):
        at = slice(h * obs, (h + 1) * obs)
        side_ref[0:1, at] = loc[h : h + 1]
        side_ref[1:2, at] = line_ref[pl.ds(table_ref[h, me], 1)]


def shards(forecast, anomalies, misfit, precision, table, tally):
    members, slots, fields, cells = forecast.shape
    used = table.shape[1]
    count, obs = misfit.shape
    table = jnp.transpose(table)
    ranks = lax.axis_size("member")
    regions = lax.axis_size("region")
    stacked = jnp.concatenate([anomalies, misfit[None]], axis=0)
    up = [(i, (i + 1) % regions) for i in range(regions)]
    edge = jax.ShapeDtypeStruct((members + 1, HW, obs), anomalies.dtype)
    tail, head = pl.pallas_call(
        edges_kernel,
        out_shape=(edge, edge),
        in_specs=[VMEM, VMEM],
        out_specs=(VMEM, VMEM),
        compiler_params=PARAMS,
        cost_estimate=pl.CostEstimate(flops=8 * 10**9, bytes_accessed=10**6, transcendentals=0),
        name="edges",
    )(stacked[:, count - HW :], stacked[:, :HW])
    before = lax.ppermute(tail, "region", up)
    after = lax.ppermute(head, "region", [(j, i) for i, j in up])
    packed, blocks = pl.pallas_call(
        pack_kernel,
        out_shape=(
            jax.ShapeDtypeStruct((slots, fields, members, cells), forecast.dtype),
            jax.ShapeDtypeStruct((count, members, obs), anomalies.dtype),
        ),
        in_specs=[VMEM] * 5,
        out_specs=(VMEM, VMEM),
        compiler_params=PARAMS,
        name="pack",
    )(table, precision, misfit, jnp.transpose(forecast, (0, 2, 1, 3)), anomalies)
    me = lax.axis_index("member").reshape(1)
    place = me + slots * (me >= tally).astype(jnp.int32)
    outgoing, side = pl.pallas_call(
        functools.partial(choose_kernel, fields),
        out_shape=(
            jax.ShapeDtypeStruct((slots, fields + used, members, cells), packed.dtype),
            jax.ShapeDtypeStruct((8, used * obs), jnp.float32),
        ),
        in_specs=[SMEM, SMEM] + [VMEM] * 6,
        out_specs=(VMEM, VMEM),
        scratch_shapes=[
            pltpu.VMEM((count + 2 * HW, members, obs), blocks.dtype),
            pltpu.VMEM((count + 2 * HW, obs), jnp.float32),
        ],
        compiler_params=PARAMS,
        name="choose",
    )(place, table, packed, blocks, precision, misfit, before, after)
    incoming = lax.all_to_all(outgoing, "member", 0, 0, tiled=True)
    back = pl.pallas_call(
        functools.partial(analyse_kernel, fields),
        out_shape=jax.ShapeDtypeStruct((ranks, fields, members, cells), forecast.dtype),
        in_specs=[VMEM, VMEM],
        out_specs=VMEM,
        compiler_params=PARAMS,
        name="analyse",
    )(incoming, side)
    back = lax.all_to_all(back, "member", 0, 0, tiled=True)
    return jnp.transpose(back, (2, 0, 1, 3))


def solution(mesh):
    return jax.shard_map(
        shards,
        mesh=mesh,
        in_specs=(
            P("member", "region", None, None),
            P("member", "region", None),
            P("region", None),
            P("region", None, None),
            P("region", None),
            P("region"),
        ),
        out_specs=P("member", "region", None, None),
        check_vma=False,
    )
```

```python
import functools
import jax
import jax.numpy as jnp
from jax import lax
from jax.experimental import pallas as pl
from jax.experimental.pallas import tpu as pltpu
from jax.sharding import PartitionSpec as P

HW = 3
NS_STEPS = 5
VMEM = pl.BlockSpec(memory_space=pltpu.VMEM)
SMEM = pl.BlockSpec(memory_space=pltpu.SMEM)
PARAMS = pltpu.CompilerParams(vmem_limit_bytes=32 * 2**20)


def split(x):
    high = x.astype(jnp.bfloat16)
    return high, (x - high.astype(jnp.float32)).astype(jnp.bfloat16)


def halves(x):
    return jnp.concatenate(split(x), axis=0)


def dot(left, right, dims=((1,), (0,))):
    return lax.dot_general(left, right, (dims, ((), ())), preferred_element_type=jnp.float32)


def narrow(left, right):
    return dot(left.astype(jnp.bfloat16), right.astype(jnp.bfloat16))


def analyse_kernel(fields, incoming_ref, side_ref, out_ref):
    ranks, blocks, members, obs = incoming_ref.shape
    lines = ranks * members

    def rows(block):
        return incoming_ref[:, block].astype(jnp.float32).reshape(lines, obs)

    def across(x):
        return jnp.sum(jnp.sum(x, axis=0, keepdims=True), axis=1, keepdims=True)

    loc, innov, live = side_ref[0:1], side_ref[1:2], side_ref[2:3, : 2 * obs] > 0
    yb = jnp.concatenate([rows(block) for block in range(fields, blocks)], axis=1)
    scaled = (yb * loc).astype(jnp.bfloat16)
    left = jnp.concatenate([yb, jnp.broadcast_to(innov, (16, yb.shape[1]))], axis=0)
    both = dot(left.astype(jnp.bfloat16), scaled, ((1,), (1,)))
    drive = both[lines : lines + 8]
    row = lax.broadcasted_iota(jnp.int32, (lines, lines), 0)
    column = lax.broadcasted_iota(jnp.int32, (lines, lines), 1)
    ident = (row == column).astype(jnp.float32)
    gram = both[:lines] * (1.0 / (lines - 1))
    amat = gram + ident
    thin, low = split(gram)
    pair = halves(drive)
    square = dot(jnp.concatenate([thin, pair], axis=0), thin)
    tail = square[lines:] + dot(pair, low)
    inverse = lax.rsqrt(across(amat * amat))
    root = jnp.sqrt(inverse)
    centre = across(amat * ident) * (1.0 / lines)

    w, n = inverse, gram * inverse
    t = 1.5 * w - 0.5 * w * w
    h = (1.5 - w) * n - (0.5 * inverse * inverse) * square[:lines]
    vector = (1.5 - 0.5 * w) * drive - (0.5 * inverse) * (tail[:8] + tail[8:])
    n = (1.5 - 0.5 * w) * h - (0.5 * t) * n - 0.5 * narrow(h, n)
    w = 1.5 * t - 0.5 * t * w
    mean = centre * inverse
    z = 1.5 - 0.5 * mean
    r = (-0.5 * inverse) * (gram - (centre - 1.0) * ident)
    mean = mean * z * z
    n = n - (mean - w) * ident
    w = mean
    for step in range(1, NS_STEPS):
        thin, low = split(n)
        last = step + 1 == NS_STEPS
        left = [r.astype(jnp.bfloat16), halves(vector)]
        both = dot(jnp.concatenate(left if last else [thin] + left, axis=0), thin)
        slope = 1.5 - 0.5 * w
        tail = both[both.shape[0] - 16 :] + dot(left[1], low)
        vector = slope * vector - 0.5 * (tail[:8] + tail[8:])
        r = slope * r - (0.5 * z) * n - 0.5 * both[both.shape[0] - 16 - lines : both.shape[0] - 16]
        z = z * slope
        if not last:
            t = slope * w
            h = (1.5 - w) * n - 0.5 * both[:lines]
            n = slope * h - (0.5 * t) * n - 0.5 * dot(h.astype(jnp.bfloat16), thin)
            w = slope * t
    high, low = split(r)
    tail = dot(halves(vector), high) + dot(halves(vector), low)
    wmean = (z * vector + (tail[:8] + tail[8:])) * (root * root * (1.0 / (lines - 1)))
    trans = (r + z * ident) * root
    weights = (trans + wmean[:1]).astype(jnp.bfloat16)
    colsum = jnp.sum(weights.astype(jnp.float32), axis=1, keepdims=True)
    for pair in range(0, fields, 2):
        field = jnp.concatenate([rows(pair), rows(pair + 1)], axis=1)
        mean = jnp.sum(field, axis=0, keepdims=True) * (1.0 / lines)
        mixed = dot(weights, field.astype(jnp.bfloat16)) + mean * (1.0 - colsum)
        mixed = jnp.where(live, mixed, field)
        for i in range(2):
            part = mixed[:, i * obs : (i + 1) * obs].reshape(ranks, members, obs)
            out_ref[:, pair + i] = part.astype(jnp.bfloat16)


def edges_kernel(tail_ref, head_ref, tail_out_ref, head_out_ref):
    tail_out_ref[...] = tail_ref[...]
    head_out_ref[...] = head_ref[...]


def pack_kernel(
    place_ref, table_ref, forecast_ref, anomalies_ref, loc_ref, misfit_ref,
    out_ref, chosen_ref, marks_ref, side_ref, blocks_ref, line_ref
):
    count, obs = misfit_ref.shape
    used, slots = table_ref.shape
    for field in range(forecast_ref.shape[1]):
        out_ref[:, field] = jnp.swapaxes(forecast_ref[:, field], 0, 1)
    blocks_ref[...] = jnp.swapaxes(anomalies_ref[...], 0, 1)
    tile = marks_ref.shape[2:]
    for slot in range(slots):
        for h in range(used):
            index = table_ref[h, slot]
            chosen_ref[slot, h] = blocks_ref[jnp.clip(index - HW, 0, count - 1)]
            marks_ref[slot, h] = jnp.full(tile, index, jnp.int32).astype(marks_ref.dtype)
    dead = place_ref[0] >= slots
    me = jnp.where(dead, place_ref[0] - slots, place_ref[0])
    line_ref[...] = misfit_ref[...].astype(jnp.float32)
    loc = loc_ref[me]
    side_ref[...] = jnp.full(side_ref.shape, jnp.where(dead, 0.0, 1.0), jnp.float32)
    for h in range(used):
        at = slice(h * obs, (h + 1) * obs)
        index = table_ref[h, me]
        side_ref[0:1, at] = loc[h : h + 1]
        side_ref[1:2, at] = line_ref[pl.ds(jnp.clip(index - HW, 0, count - 1), 1)]
        side_ref[3:4, at] = jnp.full((1, obs), index, jnp.int32).astype(jnp.float32)


def choose_kernel(
    fields, count, packed_ref, chosen_ref, marks_ref, rows_ref, before_ref, after_ref, out_ref, side_ref
):
    slots, used, members, obs = chosen_ref.shape
    out_ref[:, :fields] = packed_ref[...]
    ends = []
    for ref, first in ((before_ref, 0), (after_ref, HW + count)):
        edge = jnp.swapaxes(ref[:members], 0, 1)
        line = ref[members].astype(jnp.float32)
        ends += [(first + i, edge[i], line[i : i + 1]) for i in range(HW)]
    for h in range(used):
        marks, chosen = marks_ref[:, h], chosen_ref[:, h]
        for index, block, _ in ends:
            chosen = jnp.where(marks == jnp.bfloat16(index), block[None], chosen)
        out_ref[:, fields + h] = chosen
    side_ref[...] = rows_ref[...]
    marks, innov = rows_ref[3:4], rows_ref[1:2]
    for index, _, line in ends:
        innov = jnp.where(marks == index, jnp.concatenate([line] * used, axis=1), innov)
    side_ref[1:2] = innov


def shards(forecast, anomalies, misfit, precision, table, tally):
    members, slots, fields, cells = forecast.shape
    used = table.shape[1]
    count, obs = misfit.shape
    table = jnp.transpose(table)
    ranks = lax.axis_size("member")
    regions = lax.axis_size("region")
    stacked = jnp.concatenate([anomalies, misfit[None]], axis=0)
    up = [(i, (i + 1) % regions) for i in range(regions)]
    edge = jax.ShapeDtypeStruct((members + 1, HW, obs), anomalies.dtype)
    tail, head = pl.pallas_call(
        edges_kernel,
        out_shape=(edge, edge),
        in_specs=[VMEM, VMEM],
        out_specs=(VMEM, VMEM),
        compiler_params=PARAMS,
        cost_estimate=pl.CostEstimate(flops=8 * 10**9, bytes_accessed=10**6, transcendentals=0),
        name="edges",
    )(stacked[:, count - HW :], stacked[:, :HW])
    before = lax.ppermute(tail, "region", up)
    after = lax.ppermute(head, "region", [(j, i) for i, j in up])
    me = lax.axis_index("member").reshape(1)
    place = me + slots * (me >= tally).astype(jnp.int32)
    blocks = jax.ShapeDtypeStruct((slots, used, members, obs), anomalies.dtype)
    rows = jax.ShapeDtypeStruct((8, used * obs), jnp.float32)
    packed, chosen, marks, side = pl.pallas_call(
        pack_kernel,
        out_shape=(
            jax.ShapeDtypeStruct((slots, fields, members, cells), forecast.dtype),
            blocks,
            blocks,
            rows,
        ),
        in_specs=[SMEM, SMEM] + [VMEM] * 4,
        out_specs=(VMEM,) * 4,
        scratch_shapes=[
            pltpu.VMEM((count, members, obs), anomalies.dtype),
            pltpu.VMEM((count, obs), jnp.float32),
        ],
        compiler_params=PARAMS,
        name="pack",
    )(place, table, jnp.transpose(forecast, (0, 2, 1, 3)), anomalies, precision, misfit)
    outgoing, side = pl.pallas_call(
        functools.partial(choose_kernel, fields, count),
        out_shape=(
            jax.ShapeDtypeStruct((slots, fields + used, members, cells), packed.dtype),
            rows,
        ),
        in_specs=[VMEM] * 6,
        out_specs=(VMEM, VMEM),
        compiler_params=PARAMS,
        name="choose",
    )(packed, chosen, marks, side, before, after)
    incoming = lax.all_to_all(outgoing, "member", 0, 0, tiled=True)
    back = pl.pallas_call(
        functools.partial(analyse_kernel, fields),
        out_shape=jax.ShapeDtypeStruct((ranks, fields, members, cells), forecast.dtype),
        in_specs=[VMEM, VMEM],
        out_specs=VMEM,
        compiler_params=PARAMS,
        name="analyse",
    )(incoming, side)
    back = lax.all_to_all(back, "member", 0, 0, tiled=True)
    return jnp.transpose(back, (2, 0, 1, 3))


def solution(mesh):
    return jax.shard_map(
        shards,
        mesh=mesh,
        in_specs=(
            P("member", "region", None, None),
            P("member", "region", None),
            P("region", None),
            P("region", None, None),
            P("region", None),
            P("region"),
        ),
        out_specs=P("member", "region", None, None),
        check_vma=False,
    )
```

```python
import functools
import jax
import jax.numpy as jnp
from jax import lax
from jax.experimental import pallas as pl
from jax.experimental.pallas import tpu as pltpu
from jax.sharding import PartitionSpec as P

HW = 3
NS_STEPS = 5
VMEM = pl.BlockSpec(memory_space=pltpu.VMEM)
SMEM = pl.BlockSpec(memory_space=pltpu.SMEM)
PARAMS = pltpu.CompilerParams(vmem_limit_bytes=32 * 2**20)


def split(x):
    high = x.astype(jnp.bfloat16)
    return high, (x - high.astype(jnp.float32)).astype(jnp.bfloat16)


def halves(x):
    return jnp.concatenate(split(x), axis=0)


def dot(left, right, dims=((1,), (0,))):
    return lax.dot_general(left, right, (dims, ((), ())), preferred_element_type=jnp.float32)


def narrow(left, right):
    return dot(left.astype(jnp.bfloat16), right.astype(jnp.bfloat16))


def analyse_kernel(fields, incoming_ref, side_ref, out_ref):
    ranks, blocks, members, obs = incoming_ref.shape
    lines = ranks * members

    def rows(block):
        return incoming_ref[:, block].astype(jnp.float32).reshape(lines, obs)

    def across(x):
        return jnp.sum(jnp.sum(x, axis=0, keepdims=True), axis=1, keepdims=True)

    loc, innov, live = side_ref[0:1], side_ref[1:2], side_ref[2:3, : 2 * obs] > 0
    yb = jnp.concatenate([rows(block) for block in range(fields, blocks)], axis=1)
    scaled = (yb * loc).astype(jnp.bfloat16)
    left = jnp.concatenate([yb, jnp.broadcast_to(innov, (16, yb.shape[1]))], axis=0)
    both = dot(left.astype(jnp.bfloat16), scaled, ((1,), (1,)))
    drive = both[lines : lines + 8]
    row = lax.broadcasted_iota(jnp.int32, (lines, lines), 0)
    column = lax.broadcasted_iota(jnp.int32, (lines, lines), 1)
    ident = (row == column).astype(jnp.float32)
    gram = both[:lines] * (1.0 / (lines - 1))
    amat = gram + ident
    thin, low = split(gram)
    pair = halves(drive)
    square = dot(jnp.concatenate([thin, pair], axis=0), thin)
    tail = square[lines:] + dot(pair, low)
    inverse = lax.rsqrt(across(amat * amat))
    root = jnp.sqrt(inverse)
    centre = across(amat * ident) * (1.0 / lines)

    w, n = inverse, gram * inverse
    t = 1.5 * w - 0.5 * w * w
    h = (1.5 - w) * n - (0.5 * inverse * inverse) * square[:lines]
    vector = (1.5 - 0.5 * w) * drive - (0.5 * inverse) * (tail[:8] + tail[8:])
    n = (1.5 - 0.5 * w) * h - (0.5 * t) * n - 0.5 * narrow(h, n)
    w = 1.5 * t - 0.5 * t * w
    mean = centre * inverse
    z = 1.5 - 0.5 * mean
    r = (-0.5 * inverse) * (gram - (centre - 1.0) * ident)
    mean = mean * z * z
    n = n - (mean - w) * ident
    w = mean
    for step in range(1, NS_STEPS):
        thin, low = split(n)
        last = step + 1 == NS_STEPS
        left = [r.astype(jnp.bfloat16), halves(vector)]
        both = dot(jnp.concatenate(left if last else [thin] + left, axis=0), thin)
        slope = 1.5 - 0.5 * w
        tail = both[both.shape[0] - 16 :] + dot(left[1], low)
        vector = slope * vector - 0.5 * (tail[:8] + tail[8:])
        r = slope * r - (0.5 * z) * n - 0.5 * both[both.shape[0] - 16 - lines : both.shape[0] - 16]
        z = z * slope
        if not last:
            t = slope * w
            h = (1.5 - w) * n - 0.5 * both[:lines]
            n = slope * h - (0.5 * t) * n - 0.5 * dot(h.astype(jnp.bfloat16), thin)
            w = slope * t
    high, low = split(r)
    tail = dot(halves(vector), high) + dot(halves(vector), low)
    wmean = (z * vector + (tail[:8] + tail[8:])) * (root * root * (1.0 / (lines - 1)))
    trans = (r + z * ident) * root
    weights = (trans + wmean[:1]).astype(jnp.bfloat16)
    colsum = jnp.sum(weights.astype(jnp.float32), axis=1, keepdims=True)
    for pair in range(0, fields, 2):
        field = jnp.concatenate([rows(pair), rows(pair + 1)], axis=1)
        mean = jnp.sum(field, axis=0, keepdims=True) * (1.0 / lines)
        mixed = dot(weights, field.astype(jnp.bfloat16)) + mean * (1.0 - colsum)
        mixed = jnp.where(live, mixed, field)
        for i in range(2):
            part = mixed[:, i * obs : (i + 1) * obs].reshape(ranks, members, obs)
            out_ref[:, pair + i] = part.astype(jnp.bfloat16)


def edges_kernel(tail_ref, head_ref, tail_out_ref, head_out_ref):
    tail_out_ref[...] = tail_ref[...]
    head_out_ref[...] = head_ref[...]


def pack_kernel(
    me_ref, table_ref, forecast_ref, anomalies_ref, loc_ref, misfit_ref,
    out_ref, chosen_ref, marks_ref, side_ref, blocks_ref, line_ref
):
    count, obs = misfit_ref.shape
    used, slots = table_ref.shape[0] - 1, table_ref.shape[1]
    for field in range(forecast_ref.shape[1]):
        out_ref[:, field] = jnp.swapaxes(forecast_ref[:, field], 0, 1)
    blocks_ref[...] = jnp.swapaxes(anomalies_ref[...], 0, 1)
    tile = marks_ref.shape[2:]
    table = table_ref[...]
    for slot in range(slots):
        for h in range(used):
            index = table[h, slot]
            chosen_ref[slot, h] = blocks_ref[jnp.clip(index - HW, 0, count - 1)]
            marks_ref[slot, h] = jnp.full(tile, index, jnp.int32).astype(marks_ref.dtype)
    me = me_ref[0]
    dead = me >= table[used, 0]
    lane = lax.broadcasted_iota(jnp.int32, table.shape, 1)
    mine = jnp.sum(jnp.where(lane == me, table, 0), axis=1, keepdims=True)
    line_ref[...] = misfit_ref[...].astype(jnp.float32)
    loc = loc_ref[me]
    side_ref[...] = jnp.full(side_ref.shape, jnp.where(dead, 0.0, 1.0), jnp.float32)
    for h in range(used):
        at = slice(h * obs, (h + 1) * obs)
        index = mine[h, 0]
        side_ref[0:1, at] = loc[h : h + 1]
        side_ref[1:2, at] = line_ref[pl.ds(jnp.clip(index - HW, 0, count - 1), 1)]
        side_ref[3:4, at] = jnp.full((1, obs), index, jnp.int32).astype(jnp.float32)


def choose_kernel(
    fields, count, packed_ref, chosen_ref, marks_ref, rows_ref, before_ref, after_ref, out_ref, side_ref
):
    slots, used, members, obs = chosen_ref.shape
    out_ref[:, :fields] = packed_ref[...]
    ends = []
    for ref, first in ((before_ref, 0), (after_ref, HW + count)):
        edge = jnp.swapaxes(ref[:members], 0, 1)
        line = ref[members].astype(jnp.float32)
        ends += [(first + i, edge[i], line[i : i + 1]) for i in range(HW)]
    for h in range(used):
        marks, chosen = marks_ref[:, h], chosen_ref[:, h]
        for index, block, _ in ends:
            chosen = jnp.where(marks == jnp.bfloat16(index), block[None], chosen)
        out_ref[:, fields + h] = chosen
    side_ref[...] = rows_ref[...]
    marks, innov = rows_ref[3:4], rows_ref[1:2]
    for index, _, line in ends:
        innov = jnp.where(marks == index, jnp.concatenate([line] * used, axis=1), innov)
    side_ref[1:2] = innov


def shards(forecast, anomalies, misfit, precision, table, tally):
    members, slots, fields, cells = forecast.shape
    used = table.shape[1]
    count, obs = misfit.shape
    table = jnp.transpose(table)
    ranks = lax.axis_size("member")
    regions = lax.axis_size("region")
    stacked = jnp.concatenate([anomalies, misfit[None]], axis=0)
    up = [(i, (i + 1) % regions) for i in range(regions)]
    edge = jax.ShapeDtypeStruct((members + 1, HW, obs), anomalies.dtype)
    tail, head = pl.pallas_call(
        edges_kernel,
        out_shape=(edge, edge),
        in_specs=[VMEM, VMEM],
        out_specs=(VMEM, VMEM),
        compiler_params=PARAMS,
        cost_estimate=pl.CostEstimate(flops=8 * 10**9, bytes_accessed=10**6, transcendentals=0),
        name="edges",
    )(stacked[:, count - HW :], stacked[:, :HW])
    before = lax.ppermute(tail, "region", up)
    after = lax.ppermute(head, "region", [(j, i) for i, j in up])
    me = lax.axis_index("member").reshape(1)
    table = jnp.concatenate([table, jnp.broadcast_to(tally[None], (1, slots))], axis=0)
    blocks = jax.ShapeDtypeStruct((slots, used, members, obs), anomalies.dtype)
    rows = jax.ShapeDtypeStruct((8, used * obs), jnp.float32)
    packed, chosen, marks, side = pl.pallas_call(
        pack_kernel,
        out_shape=(
            jax.ShapeDtypeStruct((slots, fields, members, cells), forecast.dtype),
            blocks,
            blocks,
            rows,
        ),
        in_specs=[SMEM] + [VMEM] * 5,
        out_specs=(VMEM,) * 4,
        scratch_shapes=[
            pltpu.VMEM((count, members, obs), anomalies.dtype),
            pltpu.VMEM((count, obs), jnp.float32),
        ],
        compiler_params=PARAMS,
        name="pack",
    )(me, table, jnp.transpose(forecast, (0, 2, 1, 3)), anomalies, precision, misfit)
    outgoing, side = pl.pallas_call(
        functools.partial(choose_kernel, fields, count),
        out_shape=(
            jax.ShapeDtypeStruct((slots, fields + used, members, cells), packed.dtype),
            rows,
        ),
        in_specs=[VMEM] * 6,
        out_specs=(VMEM, VMEM),
        compiler_params=PARAMS,
        name="choose",
    )(packed, chosen, marks, side, before, after)
    incoming = lax.all_to_all(outgoing, "member", 0, 0, tiled=True)
    back = pl.pallas_call(
        functools.partial(analyse_kernel, fields),
        out_shape=jax.ShapeDtypeStruct((ranks, fields, members, cells), forecast.dtype),
        in_specs=[VMEM, VMEM],
        out_specs=VMEM,
        compiler_params=PARAMS,
        name="analyse",
    )(incoming, side)
    back = lax.all_to_all(back, "member", 0, 0, tiled=True)
    return jnp.transpose(back, (2, 0, 1, 3))


def solution(mesh):
    return jax.shard_map(
        shards,
        mesh=mesh,
        in_specs=(
            P("member", "region", None, None),
            P("member", "region", None),
            P("region", None),
            P("region", None, None),
            P("region", None),
            P("region"),
        ),
        out_specs=P("member", "region", None, None),
        check_vma=False,
    )
```

```python
import functools
import jax
import jax.numpy as jnp
from jax import lax
from jax.experimental import pallas as pl
from jax.experimental.pallas import tpu as pltpu
from jax.sharding import PartitionSpec as P

HW = 3
NS_STEPS = 5
VMEM = pl.BlockSpec(memory_space=pltpu.VMEM)
SMEM = pl.BlockSpec(memory_space=pltpu.SMEM)
PARAMS = pltpu.CompilerParams(vmem_limit_bytes=32 * 2**20)


def split(x):
    high = x.astype(jnp.bfloat16)
    return high, (x - high.astype(jnp.float32)).astype(jnp.bfloat16)


def halves(x):
    return jnp.concatenate(split(x), axis=0)


def dot(left, right, dims=((1,), (0,))):
    return lax.dot_general(left, right, (dims, ((), ())), preferred_element_type=jnp.float32)


def narrow(left, right):
    return dot(left.astype(jnp.bfloat16), right.astype(jnp.bfloat16))


def analyse_kernel(fields, incoming_ref, side_ref, out_ref):
    ranks, blocks, members, obs = incoming_ref.shape
    lines = ranks * members

    def rows(block):
        return incoming_ref[:, block].astype(jnp.float32).reshape(lines, obs)

    def across(x):
        return jnp.sum(jnp.sum(x, axis=0, keepdims=True), axis=1, keepdims=True)

    loc, innov, live = side_ref[0:1], side_ref[1:2], side_ref[2:3, : 2 * obs] > 0
    yb = jnp.concatenate([rows(block) for block in range(fields, blocks)], axis=1)
    scaled = (yb * loc).astype(jnp.bfloat16)
    left = jnp.concatenate([yb, jnp.broadcast_to(innov, (16, yb.shape[1]))], axis=0)
    both = dot(left.astype(jnp.bfloat16), scaled, ((1,), (1,)))
    drive = both[lines : lines + 8]
    row = lax.broadcasted_iota(jnp.int32, (lines, lines), 0)
    column = lax.broadcasted_iota(jnp.int32, (lines, lines), 1)
    ident = (row == column).astype(jnp.float32)
    gram = both[:lines] * (1.0 / (lines - 1))
    amat = gram + ident
    thin, low = split(gram)
    pair = halves(drive)
    square = dot(jnp.concatenate([thin, pair], axis=0), thin)
    tail = square[lines:] + dot(pair, low)
    inverse = lax.rsqrt(across(amat * amat))
    root = jnp.sqrt(inverse)
    centre = across(amat * ident) * (1.0 / lines)

    w, n = inverse, gram * inverse
    t = 1.5 * w - 0.5 * w * w
    h = (1.5 - w) * n - (0.5 * inverse * inverse) * square[:lines]
    vector = (1.5 - 0.5 * w) * drive - (0.5 * inverse) * (tail[:8] + tail[8:])
    n = (1.5 - 0.5 * w) * h - (0.5 * t) * n - 0.5 * narrow(h, n)
    w = 1.5 * t - 0.5 * t * w
    mean = centre * inverse
    z = 1.5 - 0.5 * mean
    r = (-0.5 * inverse) * (gram - (centre - 1.0) * ident)
    mean = mean * z * z
    n = n - (mean - w) * ident
    w = mean
    for step in range(1, NS_STEPS):
        thin, low = split(n)
        last = step + 1 == NS_STEPS
        left = [r.astype(jnp.bfloat16), halves(vector)]
        both = dot(jnp.concatenate(left if last else [thin] + left, axis=0), thin)
        slope = 1.5 - 0.5 * w
        tail = both[both.shape[0] - 16 :] + dot(left[1], low)
        vector = slope * vector - 0.5 * (tail[:8] + tail[8:])
        r = slope * r - (0.5 * z) * n - 0.5 * both[both.shape[0] - 16 - lines : both.shape[0] - 16]
        z = z * slope
        if not last:
            t = slope * w
            h = (1.5 - w) * n - 0.5 * both[:lines]
            n = slope * h - (0.5 * t) * n - 0.5 * dot(h.astype(jnp.bfloat16), thin)
            w = slope * t
    high, low = split(r)
    tail = dot(halves(vector), high) + dot(halves(vector), low)
    wmean = (z * vector + (tail[:8] + tail[8:])) * (root * root * (1.0 / (lines - 1)))
    trans = (r + z * ident) * root
    weights = (trans + wmean[:1]).astype(jnp.bfloat16)
    colsum = jnp.sum(weights.astype(jnp.float32), axis=1, keepdims=True)
    for pair in range(0, fields, 2):
        field = jnp.concatenate([rows(pair), rows(pair + 1)], axis=1)
        mean = jnp.sum(field, axis=0, keepdims=True) * (1.0 / lines)
        mixed = dot(weights, field.astype(jnp.bfloat16)) + mean * (1.0 - colsum)
        mixed = jnp.where(live, mixed, field)
        for i in range(2):
            part = mixed[:, i * obs : (i + 1) * obs].reshape(ranks, members, obs)
            out_ref[:, pair + i] = part.astype(jnp.bfloat16)


def edges_kernel(tail_ref, head_ref, tail_out_ref, head_out_ref):
    tail_out_ref[...] = tail_ref[...]
    head_out_ref[...] = head_ref[...]


def pack_kernel(
    me_ref, table_ref, forecast_ref, anomalies_ref, loc_ref, misfit_ref,
    out_ref, chosen_ref, marks_ref, side_ref, blocks_ref, line_ref
):
    count, obs = misfit_ref.shape
    used, slots = table_ref.shape[0] - 1, table_ref.shape[1]
    for field in range(forecast_ref.shape[1]):
        out_ref[:, field] = jnp.swapaxes(forecast_ref[:, field], 0, 1)
    blocks_ref[...] = jnp.swapaxes(anomalies_ref[...], 0, 1)
    tile = marks_ref.shape[2:]
    table = table_ref[...]
    for slot in range(slots):
        for h in range(used):
            index = table[h, slot]
            chosen_ref[slot, h] = blocks_ref[jnp.clip(index - HW, 0, count - 1)]
            marks_ref[slot, h] = jnp.full(tile, index, jnp.int32).astype(marks_ref.dtype)
    me = me_ref[0]
    dead = me >= table[used, 0]
    lane = lax.broadcasted_iota(jnp.int32, table.shape, 1)
    mine = jnp.sum(jnp.where(lane == me, table, 0), axis=1, keepdims=True)
    line_ref[...] = misfit_ref[...].astype(jnp.float32)
    loc = loc_ref[me]
    side_ref[...] = jnp.full(side_ref.shape, jnp.where(dead, 0.0, 1.0), jnp.float32)
    for h in range(used):
        at = slice(h * obs, (h + 1) * obs)
        index = mine[h, 0]
        side_ref[0:1, at] = loc[h : h + 1]
        side_ref[1:2, at] = line_ref[pl.ds(jnp.clip(index - HW, 0, count - 1), 1)]
        side_ref[3:4, at] = jnp.full((1, obs), index, jnp.int32).astype(jnp.float32)


def choose_kernel(
    fields, count, packed_ref, chosen_ref, marks_ref, rows_ref, before_ref, after_ref, out_ref, side_ref
):
    slots, used, members, obs = chosen_ref.shape
    out_ref[:, :fields] = packed_ref[...]
    ends = []
    for ref, first in ((before_ref, 0), (after_ref, HW + count)):
        edge = jnp.swapaxes(ref[:members], 0, 1)
        line = ref[members].astype(jnp.float32)
        ends += [(first + i, edge[i], line[i : i + 1]) for i in range(HW)]
    for h in range(used):
        marks, chosen = marks_ref[:, h], chosen_ref[:, h]
        for index, block, _ in ends:
            chosen = jnp.where(marks == jnp.bfloat16(index), block[None], chosen)
        out_ref[:, fields + h] = chosen
    side_ref[...] = rows_ref[...]
    marks, innov = rows_ref[3:4], rows_ref[1:2]
    for index, _, line in ends:
        innov = jnp.where(marks == index, jnp.concatenate([line] * used, axis=1), innov)
    side_ref[1:2] = innov


def shards(forecast, anomalies, misfit, precision, table, tally):
    members, slots, fields, cells = forecast.shape
    used = table.shape[1]
    count, obs = misfit.shape
    table = jnp.transpose(table)
    ranks = lax.axis_size("member")
    regions = lax.axis_size("region")
    stacked = jnp.concatenate([anomalies, misfit[None]], axis=0)
    up = [(i, (i + 1) % regions) for i in range(regions)]
    edge = jax.ShapeDtypeStruct((members + 1, HW, obs), anomalies.dtype)
    tail, head = pl.pallas_call(
        edges_kernel,
        out_shape=(edge, edge),
        in_specs=[VMEM, VMEM],
        out_specs=(VMEM, VMEM),
        compiler_params=PARAMS,
        cost_estimate=pl.CostEstimate(flops=8 * 10**9, bytes_accessed=10**6, transcendentals=0),
        name="edges",
    )(stacked[:, count - HW :], stacked[:, :HW])
    before = lax.ppermute(tail, "region", up)
    after = lax.ppermute(head, "region", [(j, i) for i, j in up])
    order = [ranks - 1 - i for i in range(ranks)]
    me = lax.axis_index("member").reshape(1)
    me = ranks - 1 - me
    table = jnp.concatenate([table, jnp.broadcast_to(tally[None], (1, slots))], axis=0)
    blocks = jax.ShapeDtypeStruct((slots, used, members, obs), anomalies.dtype)
    rows = jax.ShapeDtypeStruct((8, used * obs), jnp.float32)
    packed, chosen, marks, side = pl.pallas_call(
        pack_kernel,
        out_shape=(
            jax.ShapeDtypeStruct((slots, fields, members, cells), forecast.dtype),
            blocks,
            blocks,
            rows,
        ),
        in_specs=[SMEM] + [VMEM] * 5,
        out_specs=(VMEM,) * 4,
        scratch_shapes=[
            pltpu.VMEM((count, members, obs), anomalies.dtype),
            pltpu.VMEM((count, obs), jnp.float32),
        ],
        compiler_params=PARAMS,
        name="pack",
    )(me, table, jnp.transpose(forecast, (0, 2, 1, 3)), anomalies, precision, misfit)
    outgoing, side = pl.pallas_call(
        functools.partial(choose_kernel, fields, count),
        out_shape=(
            jax.ShapeDtypeStruct((slots, fields + used, members, cells), packed.dtype),
            rows,
        ),
        in_specs=[VMEM] * 6,
        out_specs=(VMEM, VMEM),
        compiler_params=PARAMS,
        name="choose",
    )(packed, chosen, marks, side, before, after)
    incoming = lax.all_to_all(outgoing, "member", 0, 0, tiled=True, axis_index_groups=[order])
    back = pl.pallas_call(
        functools.partial(analyse_kernel, fields),
        out_shape=jax.ShapeDtypeStruct((ranks, fields, members, cells), forecast.dtype),
        in_specs=[VMEM, VMEM],
        out_specs=VMEM,
        compiler_params=PARAMS,
        name="analyse",
    )(incoming, side)
    back = lax.all_to_all(back, "member", 0, 0, tiled=True, axis_index_groups=[order])
    return jnp.transpose(back, (2, 0, 1, 3))


def solution(mesh):
    return jax.shard_map(
        shards,
        mesh=mesh,
        in_specs=(
            P("member", "region", None, None),
            P("member", "region", None),
            P("region", None),
            P("region", None, None),
            P("region", None),
            P("region"),
        ),
        out_specs=P("member", "region", None, None),
        check_vma=False,
    )
```

```python
import functools
import jax
import jax.numpy as jnp
from jax import lax
from jax.experimental import pallas as pl
from jax.experimental.pallas import tpu as pltpu
from jax.sharding import PartitionSpec as P

HW = 3
NS_STEPS = 5
VMEM = pl.BlockSpec(memory_space=pltpu.VMEM)
SMEM = pl.BlockSpec(memory_space=pltpu.SMEM)
PARAMS = pltpu.CompilerParams(vmem_limit_bytes=32 * 2**20)


def split(x):
    high = x.astype(jnp.bfloat16)
    return high, (x - high.astype(jnp.float32)).astype(jnp.bfloat16)


def halves(x):
    return jnp.concatenate(split(x), axis=0)


def dot(left, right, dims=((1,), (0,))):
    return lax.dot_general(left, right, (dims, ((), ())), preferred_element_type=jnp.float32)


def narrow(left, right):
    return dot(left.astype(jnp.bfloat16), right.astype(jnp.bfloat16))


def analyse_kernel(fields, incoming_ref, side_ref, out_ref):
    ranks, blocks, members, obs = incoming_ref.shape
    lines = ranks * members

    def rows(block):
        return incoming_ref[:, block].astype(jnp.float32).reshape(lines, obs)

    def across(x):
        return jnp.sum(jnp.sum(x, axis=0, keepdims=True), axis=1, keepdims=True)

    loc, innov, live = side_ref[0:1], side_ref[1:2], side_ref[2:3, : 2 * obs] > 0
    yb = jnp.concatenate([rows(block) for block in range(fields, blocks)], axis=1)
    scaled = (yb * loc).astype(jnp.bfloat16)
    left = jnp.concatenate([yb, jnp.broadcast_to(innov, (16, yb.shape[1]))], axis=0)
    both = dot(left.astype(jnp.bfloat16), scaled, ((1,), (1,)))
    drive = both[lines : lines + 8]
    row = lax.broadcasted_iota(jnp.int32, (lines, lines), 0)
    column = lax.broadcasted_iota(jnp.int32, (lines, lines), 1)
    ident = (row == column).astype(jnp.float32)
    gram = both[:lines] * (1.0 / (lines - 1))
    amat = gram + ident
    thin, low = split(gram)
    pair = halves(drive)
    square = dot(jnp.concatenate([thin, pair], axis=0), thin)
    tail = square[lines:] + dot(pair, low)
    inverse = lax.rsqrt(across(amat * amat))
    root = jnp.sqrt(inverse)
    centre = across(amat * ident) * (1.0 / lines)

    w, n = inverse, gram * inverse
    t = 1.5 * w - 0.5 * w * w
    h = (1.5 - w) * n - (0.5 * inverse * inverse) * square[:lines]
    vector = (1.5 - 0.5 * w) * drive - (0.5 * inverse) * (tail[:8] + tail[8:])
    n = (1.5 - 0.5 * w) * h - (0.5 * t) * n - 0.5 * narrow(h, n)
    w = 1.5 * t - 0.5 * t * w
    mean = centre * inverse
    z = 1.5 - 0.5 * mean
    r = (-0.5 * inverse) * (gram - (centre - 1.0) * ident)
    mean = mean * z * z
    n = n - (mean - w) * ident
    w = mean
    for step in range(1, NS_STEPS):
        thin, low = split(n)
        last = step + 1 == NS_STEPS
        left = [r.astype(jnp.bfloat16), halves(vector)]
        both = dot(jnp.concatenate(left if last else [thin] + left, axis=0), thin)
        slope = 1.5 - 0.5 * w
        tail = both[both.shape[0] - 16 :] + dot(left[1], low)
        vector = slope * vector - 0.5 * (tail[:8] + tail[8:])
        r = slope * r - (0.5 * z) * n - 0.5 * both[both.shape[0] - 16 - lines : both.shape[0] - 16]
        z = z * slope
        if not last:
            t = slope * w
            h = (1.5 - w) * n - 0.5 * both[:lines]
            n = slope * h - (0.5 * t) * n - 0.5 * dot(h.astype(jnp.bfloat16), thin)
            w = slope * t
    high, low = split(r)
    tail = dot(halves(vector), high) + dot(halves(vector), low)
    wmean = (z * vector + (tail[:8] + tail[8:])) * (root * root * (1.0 / (lines - 1)))
    trans = (r + z * ident) * root
    weights = (trans + wmean[:1]).astype(jnp.bfloat16)
    colsum = jnp.sum(weights.astype(jnp.float32), axis=1, keepdims=True)
    for pair in range(0, fields, 2):
        field = jnp.concatenate([rows(pair), rows(pair + 1)], axis=1)
        mean = jnp.sum(field, axis=0, keepdims=True) * (1.0 / lines)
        mixed = dot(weights, field.astype(jnp.bfloat16)) + mean * (1.0 - colsum)
        mixed = jnp.where(live, mixed, field)
        for i in range(2):
            part = mixed[:, i * obs : (i + 1) * obs].reshape(ranks, members, obs)
            out_ref[:, pair + i] = part.astype(jnp.bfloat16)


def edges_kernel(tail_ref, head_ref, tail_out_ref, head_out_ref):
    tail_out_ref[...] = tail_ref[...]
    head_out_ref[...] = head_ref[...]


def pack_kernel(
    me_ref, table_ref, forecast_ref, anomalies_ref, loc_ref, misfit_ref,
    out_ref, chosen_ref, marks_ref, side_ref, blocks_ref, line_ref
):
    count, obs = misfit_ref.shape
    used, slots = table_ref.shape[0] - 1, table_ref.shape[1]
    for field in range(forecast_ref.shape[1]):
        out_ref[:, field] = jnp.swapaxes(forecast_ref[:, field], 0, 1)
    blocks_ref[...] = jnp.swapaxes(anomalies_ref[...], 0, 1)
    tile = marks_ref.shape[2:]
    table = table_ref[...]
    for slot in range(slots):
        for h in range(used):
            index = table[h, slot]
            chosen_ref[slot, h] = blocks_ref[jnp.clip(index - HW, 0, count - 1)]
            marks_ref[slot, h] = jnp.full(tile, index, jnp.int32).astype(marks_ref.dtype)
    me = me_ref[0]
    dead = me >= table[used, 0]
    lane = lax.broadcasted_iota(jnp.int32, table.shape, 1)
    mine = jnp.sum(jnp.where(lane == me, table, 0), axis=1, keepdims=True)
    line_ref[...] = misfit_ref[...].astype(jnp.float32)
    loc = loc_ref[me]
    side_ref[...] = jnp.full(side_ref.shape, jnp.where(dead, 0.0, 1.0), jnp.float32)
    for h in range(used):
        at = slice(h * obs, (h + 1) * obs)
        index = mine[h, 0]
        side_ref[0:1, at] = loc[h : h + 1]
        side_ref[1:2, at] = line_ref[pl.ds(jnp.clip(index - HW, 0, count - 1), 1)]
        side_ref[3:4, at] = jnp.full((1, obs), index, jnp.int32).astype(jnp.float32)


def choose_kernel(
    fields, count, packed_ref, chosen_ref, marks_ref, rows_ref, before_ref, after_ref, out_ref, side_ref
):
    slots, used, members, obs = chosen_ref.shape
    out_ref[:, :fields] = packed_ref[...]
    ends = []
    for ref, first in ((before_ref, 0), (after_ref, HW + count)):
        edge = jnp.swapaxes(ref[:members], 0, 1)
        line = ref[members].astype(jnp.float32)
        ends += [(first + i, edge[i], line[i : i + 1]) for i in range(HW)]
    for h in range(used):
        marks, chosen = marks_ref[:, h], chosen_ref[:, h]
        for index, block, _ in ends:
            chosen = jnp.where(marks == jnp.bfloat16(index), block[None], chosen)
        out_ref[:, fields + h] = chosen
    side_ref[...] = rows_ref[...]
    marks, innov = rows_ref[3:4], rows_ref[1:2]
    for index, _, line in ends:
        innov = jnp.where(marks == index, jnp.concatenate([line] * used, axis=1), innov)
    side_ref[1:2] = innov


def shards(forecast, anomalies, misfit, precision, table, tally):
    members, slots, fields, cells = forecast.shape
    used = table.shape[1]
    count, obs = misfit.shape
    table = jnp.transpose(table)
    ranks = lax.axis_size("member")
    regions = lax.axis_size("region")
    stacked = jnp.concatenate([anomalies, misfit[None]], axis=0)
    up = [(i, (i + 1) % regions) for i in range(regions)]
    edge = jax.ShapeDtypeStruct((members + 1, HW, obs), anomalies.dtype)
    tail, head = pl.pallas_call(
        edges_kernel,
        out_shape=(edge, edge),
        in_specs=[VMEM, VMEM],
        out_specs=(VMEM, VMEM),
        compiler_params=PARAMS,
        cost_estimate=pl.CostEstimate(flops=8 * 10**9, bytes_accessed=10**6, transcendentals=0),
        name="edges",
    )(stacked[:, count - HW :], stacked[:, :HW])
    before = lax.ppermute(tail, "region", up)
    after = lax.ppermute(head, "region", [(j, i) for i, j in up])
    order = [(27 - i) % ranks for i in range(ranks)]
    me = lax.axis_index("member").reshape(1)
    me = (27 - me + ranks) % ranks
    table = jnp.concatenate([table, jnp.broadcast_to(tally[None], (1, slots))], axis=0)
    blocks = jax.ShapeDtypeStruct((slots, used, members, obs), anomalies.dtype)
    rows = jax.ShapeDtypeStruct((8, used * obs), jnp.float32)
    packed, chosen, marks, side = pl.pallas_call(
        pack_kernel,
        out_shape=(
            jax.ShapeDtypeStruct((slots, fields, members, cells), forecast.dtype),
            blocks,
            blocks,
            rows,
        ),
        in_specs=[SMEM] + [VMEM] * 5,
        out_specs=(VMEM,) * 4,
        scratch_shapes=[
            pltpu.VMEM((count, members, obs), anomalies.dtype),
            pltpu.VMEM((count, obs), jnp.float32),
        ],
        compiler_params=PARAMS,
        name="pack",
    )(me, table, jnp.transpose(forecast, (0, 2, 1, 3)), anomalies, precision, misfit)
    outgoing, side = pl.pallas_call(
        functools.partial(choose_kernel, fields, count),
        out_shape=(
            jax.ShapeDtypeStruct((slots, fields + used, members, cells), packed.dtype),
            rows,
        ),
        in_specs=[VMEM] * 6,
        out_specs=(VMEM, VMEM),
        compiler_params=PARAMS,
        name="choose",
    )(packed, chosen, marks, side, before, after)
    incoming = lax.all_to_all(outgoing, "member", 0, 0, tiled=True, axis_index_groups=[order])
    back = pl.pallas_call(
        functools.partial(analyse_kernel, fields),
        out_shape=jax.ShapeDtypeStruct((ranks, fields, members, cells), forecast.dtype),
        in_specs=[VMEM, VMEM],
        out_specs=VMEM,
        compiler_params=PARAMS,
        name="analyse",
    )(incoming, side)
    back = lax.all_to_all(back, "member", 0, 0, tiled=True, axis_index_groups=[order])
    return jnp.transpose(back, (2, 0, 1, 3))


def solution(mesh):
    return jax.shard_map(
        shards,
        mesh=mesh,
        in_specs=(
            P("member", "region", None, None),
            P("member", "region", None),
            P("region", None),
            P("region", None, None),
            P("region", None),
            P("region"),
        ),
        out_specs=P("member", "region", None, None),
        check_vma=False,
    )
```

```python
import functools
import jax
import jax.numpy as jnp
from jax import lax
from jax.experimental import pallas as pl
from jax.experimental.pallas import tpu as pltpu
from jax.sharding import PartitionSpec as P

HW = 3
NS_STEPS = 5
VMEM = pl.BlockSpec(memory_space=pltpu.VMEM)
SMEM = pl.BlockSpec(memory_space=pltpu.SMEM)
PARAMS = pltpu.CompilerParams(vmem_limit_bytes=32 * 2**20)


def split(x):
    high = x.astype(jnp.bfloat16)
    return high, (x - high.astype(jnp.float32)).astype(jnp.bfloat16)


def halves(x):
    return jnp.concatenate(split(x), axis=0)


def dot(left, right, dims=((1,), (0,))):
    return lax.dot_general(left, right, (dims, ((), ())), preferred_element_type=jnp.float32)


def narrow(left, right):
    return dot(left.astype(jnp.bfloat16), right.astype(jnp.bfloat16))


def analyse_kernel(fields, incoming_ref, side_ref, out_ref):
    ranks, blocks, members, obs = incoming_ref.shape
    lines = ranks * members

    def rows(block):
        return incoming_ref[:, block].astype(jnp.float32).reshape(lines, obs)

    def across(x):
        return jnp.sum(jnp.sum(x, axis=0, keepdims=True), axis=1, keepdims=True)

    loc, innov, live = side_ref[0:1], side_ref[1:2], side_ref[2:3, : 2 * obs] > 0
    yb = jnp.concatenate([rows(block) for block in range(fields, blocks)], axis=1)
    scaled = (yb * loc).astype(jnp.bfloat16)
    left = jnp.concatenate([yb, jnp.broadcast_to(innov, (16, yb.shape[1]))], axis=0)
    both = dot(left.astype(jnp.bfloat16), scaled, ((1,), (1,)))
    drive = both[lines : lines + 8]
    row = lax.broadcasted_iota(jnp.int32, (lines, lines), 0)
    column = lax.broadcasted_iota(jnp.int32, (lines, lines), 1)
    ident = (row == column).astype(jnp.float32)
    gram = both[:lines] * (1.0 / (lines - 1))
    amat = gram + ident
    thin, low = split(gram)
    pair = halves(drive)
    square = dot(jnp.concatenate([thin, pair], axis=0), thin)
    tail = square[lines:] + dot(pair, low)
    inverse = lax.rsqrt(across(amat * amat))
    root = jnp.sqrt(inverse)
    centre = across(amat * ident) * (1.0 / lines)

    w, n = inverse, gram * inverse
    t = 1.5 * w - 0.5 * w * w
    h = (1.5 - w) * n - (0.5 * inverse * inverse) * square[:lines]
    vector = (1.5 - 0.5 * w) * drive - (0.5 * inverse) * (tail[:8] + tail[8:])
    n = (1.5 - 0.5 * w) * h - (0.5 * t) * n - 0.5 * narrow(h, n)
    w = 1.5 * t - 0.5 * t * w
    mean = centre * inverse
    z = 1.5 - 0.5 * mean
    r = (-0.5 * inverse) * (gram - (centre - 1.0) * ident)
    mean = mean * z * z
    n = n - (mean - w) * ident
    w = mean
    for step in range(1, NS_STEPS):
        thin, low = split(n)
        last = step + 1 == NS_STEPS
        left = [r.astype(jnp.bfloat16), halves(vector)]
        both = dot(jnp.concatenate(left if last else [thin] + left, axis=0), thin)
        slope = 1.5 - 0.5 * w
        tail = both[both.shape[0] - 16 :] + dot(left[1], low)
        vector = slope * vector - 0.5 * (tail[:8] + tail[8:])
        r = slope * r - (0.5 * z) * n - 0.5 * both[both.shape[0] - 16 - lines : both.shape[0] - 16]
        z = z * slope
        if not last:
            t = slope * w
            h = (1.5 - w) * n - 0.5 * both[:lines]
            n = slope * h - (0.5 * t) * n - 0.5 * dot(h.astype(jnp.bfloat16), thin)
            w = slope * t
    high, low = split(r)
    tail = dot(halves(vector), high) + dot(halves(vector), low)
    wmean = (z * vector + (tail[:8] + tail[8:])) * (root * root * (1.0 / (lines - 1)))
    trans = (r + z * ident) * root
    weights = (trans + wmean[:1]).astype(jnp.bfloat16)
    colsum = jnp.sum(weights.astype(jnp.float32), axis=1, keepdims=True)
    for pair in range(0, fields, 2):
        field = jnp.concatenate([rows(pair), rows(pair + 1)], axis=1)
        mean = jnp.sum(field, axis=0, keepdims=True) * (1.0 / lines)
        mixed = dot(weights, field.astype(jnp.bfloat16)) + mean * (1.0 - colsum)
        mixed = jnp.where(live, mixed, field)
        for i in range(2):
            part = mixed[:, i * obs : (i + 1) * obs].reshape(ranks, members, obs)
            out_ref[:, pair + i] = part.astype(jnp.bfloat16)


def edges_kernel(tail_ref, head_ref, tail_out_ref, head_out_ref):
    tail_out_ref[...] = tail_ref[...]
    head_out_ref[...] = head_ref[...]


def pack_kernel(
    me_ref, table_ref, forecast_ref, anomalies_ref, loc_ref, misfit_ref,
    out_ref, chosen_ref, marks_ref, side_ref, blocks_ref, line_ref
):
    count, obs = misfit_ref.shape
    used, slots = table_ref.shape[0] - 1, table_ref.shape[1]
    for field in range(forecast_ref.shape[1]):
        out_ref[:, field] = jnp.swapaxes(forecast_ref[:, field], 0, 1)
    blocks_ref[...] = jnp.swapaxes(anomalies_ref[...], 0, 1)
    tile = marks_ref.shape[2:]
    table = table_ref[...]
    for slot in range(slots):
        for h in range(used):
            index = table[h, slot]
            chosen_ref[slot, h] = blocks_ref[jnp.clip(index - HW, 0, count - 1)]
            marks_ref[slot, h] = jnp.full(tile, index, jnp.int32).astype(marks_ref.dtype)
    me = me_ref[0]
    dead = me >= table[used, 0]
    lane = lax.broadcasted_iota(jnp.int32, table.shape, 1)
    mine = jnp.sum(jnp.where(lane == me, table, 0), axis=1, keepdims=True)
    line_ref[...] = misfit_ref[...].astype(jnp.float32)
    loc = loc_ref[me]
    side_ref[...] = jnp.full(side_ref.shape, jnp.where(dead, 0.0, 1.0), jnp.float32)
    for h in range(used):
        at = slice(h * obs, (h + 1) * obs)
        index = mine[h, 0]
        side_ref[0:1, at] = loc[h : h + 1]
        side_ref[1:2, at] = line_ref[pl.ds(jnp.clip(index - HW, 0, count - 1), 1)]
        side_ref[3:4, at] = jnp.full((1, obs), index, jnp.int32).astype(jnp.float32)


def choose_kernel(
    fields, count, packed_ref, chosen_ref, marks_ref, rows_ref, before_ref, after_ref, out_ref, side_ref
):
    slots, used, members, obs = chosen_ref.shape
    out_ref[:, :fields] = packed_ref[...]
    ends = []
    for ref, first in ((before_ref, 0), (after_ref, HW + count)):
        edge = jnp.swapaxes(ref[:members], 0, 1)
        line = ref[members].astype(jnp.float32)
        ends += [(first + i, edge[i], line[i : i + 1]) for i in range(HW)]
    for h in range(used):
        marks, chosen = marks_ref[:, h], chosen_ref[:, h]
        for index, block, _ in ends:
            chosen = jnp.where(marks == jnp.bfloat16(index), block[None], chosen)
        out_ref[:, fields + h] = chosen
    side_ref[...] = rows_ref[...]
    marks, innov = rows_ref[3:4], rows_ref[1:2]
    for index, _, line in ends:
        innov = jnp.where(marks == index, jnp.concatenate([line] * used, axis=1), innov)
    side_ref[1:2] = innov


def shards(forecast, anomalies, misfit, precision, table, tally):
    members, slots, fields, cells = forecast.shape
    used = table.shape[1]
    count, obs = misfit.shape
    table = jnp.transpose(table)
    ranks = lax.axis_size("member")
    regions = lax.axis_size("region")
    stacked = jnp.concatenate([anomalies, misfit[None]], axis=0)
    up = [(i, (i + 1) % regions) for i in range(regions)]
    edge = jax.ShapeDtypeStruct((members + 1, HW, obs), anomalies.dtype)
    tail, head = pl.pallas_call(
        edges_kernel,
        out_shape=(edge, edge),
        in_specs=[VMEM, VMEM],
        out_specs=(VMEM, VMEM),
        compiler_params=PARAMS,
        cost_estimate=pl.CostEstimate(flops=8 * 10**9, bytes_accessed=10**6, transcendentals=0),
        name="edges",
    )(stacked[:, count - HW :], stacked[:, :HW])
    before = lax.ppermute(tail, "region", up)
    after = lax.ppermute(head, "region", [(j, i) for i, j in up])
    order = [(25 - i) % ranks for i in range(ranks)]
    me = lax.axis_index("member").reshape(1)
    me = (25 - me + ranks) % ranks
    table = jnp.concatenate([table, jnp.broadcast_to(tally[None], (1, slots))], axis=0)
    blocks = jax.ShapeDtypeStruct((slots, used, members, obs), anomalies.dtype)
    rows = jax.ShapeDtypeStruct((8, used * obs), jnp.float32)
    packed, chosen, marks, side = pl.pallas_call(
        pack_kernel,
        out_shape=(
            jax.ShapeDtypeStruct((slots, fields, members, cells), forecast.dtype),
            blocks,
            blocks,
            rows,
        ),
        in_specs=[SMEM] + [VMEM] * 5,
        out_specs=(VMEM,) * 4,
        scratch_shapes=[
            pltpu.VMEM((count, members, obs), anomalies.dtype),
            pltpu.VMEM((count, obs), jnp.float32),
        ],
        compiler_params=PARAMS,
        name="pack",
    )(me, table, jnp.transpose(forecast, (0, 2, 1, 3)), anomalies, precision, misfit)
    outgoing, side = pl.pallas_call(
        functools.partial(choose_kernel, fields, count),
        out_shape=(
            jax.ShapeDtypeStruct((slots, fields + used, members, cells), packed.dtype),
            rows,
        ),
        in_specs=[VMEM] * 6,
        out_specs=(VMEM, VMEM),
        compiler_params=PARAMS,
        name="choose",
    )(packed, chosen, marks, side, before, after)
    incoming = lax.all_to_all(outgoing, "member", 0, 0, tiled=True, axis_index_groups=[order])
    back = pl.pallas_call(
        functools.partial(analyse_kernel, fields),
        out_shape=jax.ShapeDtypeStruct((ranks, fields, members, cells), forecast.dtype),
        in_specs=[VMEM, VMEM],
        out_specs=VMEM,
        compiler_params=PARAMS,
        name="analyse",
    )(incoming, side)
    back = lax.all_to_all(back, "member", 0, 0, tiled=True, axis_index_groups=[order])
    return jnp.transpose(back, (2, 0, 1, 3))


def solution(mesh):
    return jax.shard_map(
        shards,
        mesh=mesh,
        in_specs=(
            P("member", "region", None, None),
            P("member", "region", None),
            P("region", None),
            P("region", None, None),
            P("region", None),
            P("region"),
        ),
        out_specs=P("member", "region", None, None),
        check_vma=False,
    )
```

```python
import functools
import jax
import jax.numpy as jnp
from jax import lax
from jax.experimental import pallas as pl
from jax.experimental.pallas import tpu as pltpu
from jax.sharding import PartitionSpec as P

HW = 3
NS_STEPS = 5
VMEM = pl.BlockSpec(memory_space=pltpu.VMEM)
SMEM = pl.BlockSpec(memory_space=pltpu.SMEM)
PARAMS = pltpu.CompilerParams(vmem_limit_bytes=32 * 2**20)


def split(x):
    high = x.astype(jnp.bfloat16)
    return high, (x - high.astype(jnp.float32)).astype(jnp.bfloat16)


def halves(x):
    return jnp.concatenate(split(x), axis=0)


def dot(left, right, dims=((1,), (0,))):
    return lax.dot_general(left, right, (dims, ((), ())), preferred_element_type=jnp.float32)


def narrow(left, right):
    return dot(left.astype(jnp.bfloat16), right.astype(jnp.bfloat16))


def analyse_kernel(fields, incoming_ref, side_ref, out_ref):
    ranks, blocks, members, obs = incoming_ref.shape
    lines = ranks * members

    def rows(block):
        return incoming_ref[:, block].astype(jnp.float32).reshape(lines, obs)

    def across(x):
        return jnp.sum(jnp.sum(x, axis=0, keepdims=True), axis=1, keepdims=True)

    loc, innov, live = side_ref[0:1], side_ref[1:2], side_ref[2:3, : 2 * obs] > 0
    yb = jnp.concatenate([rows(block) for block in range(fields, blocks)], axis=1)
    scaled = (yb * loc).astype(jnp.bfloat16)
    left = jnp.concatenate([yb, jnp.broadcast_to(innov, (16, yb.shape[1]))], axis=0)
    both = dot(left.astype(jnp.bfloat16), scaled, ((1,), (1,)))
    drive = both[lines : lines + 8]
    row = lax.broadcasted_iota(jnp.int32, (lines, lines), 0)
    column = lax.broadcasted_iota(jnp.int32, (lines, lines), 1)
    ident = (row == column).astype(jnp.float32)
    gram = both[:lines] * (1.0 / (lines - 1))
    amat = gram + ident
    thin, low = split(gram)
    pair = halves(drive)
    square = dot(jnp.concatenate([thin, pair], axis=0), thin)
    tail = square[lines:] + dot(pair, low)
    inverse = lax.rsqrt(across(amat * amat))
    root = jnp.sqrt(inverse)
    centre = across(amat * ident) * (1.0 / lines)

    w, n = inverse, gram * inverse
    t = 1.5 * w - 0.5 * w * w
    h = (1.5 - w) * n - (0.5 * inverse * inverse) * square[:lines]
    vector = (1.5 - 0.5 * w) * drive - (0.5 * inverse) * (tail[:8] + tail[8:])
    n = (1.5 - 0.5 * w) * h - (0.5 * t) * n - 0.5 * narrow(h, n)
    w = 1.5 * t - 0.5 * t * w
    mean = centre * inverse
    z = 1.5 - 0.5 * mean
    r = (-0.5 * inverse) * (gram - (centre - 1.0) * ident)
    mean = mean * z * z
    n = n - (mean - w) * ident
    w = mean
    for step in range(1, NS_STEPS):
        thin, low = split(n)
        last = step + 1 == NS_STEPS
        left = [r.astype(jnp.bfloat16), halves(vector)]
        both = dot(jnp.concatenate(left if last else [thin] + left, axis=0), thin)
        slope = 1.5 - 0.5 * w
        tail = both[both.shape[0] - 16 :] + dot(left[1], low)
        vector = slope * vector - 0.5 * (tail[:8] + tail[8:])
        r = slope * r - (0.5 * z) * n - 0.5 * both[both.shape[0] - 16 - lines : both.shape[0] - 16]
        z = z * slope
        if not last:
            t = slope * w
            h = (1.5 - w) * n - 0.5 * both[:lines]
            n = slope * h - (0.5 * t) * n - 0.5 * dot(h.astype(jnp.bfloat16), thin)
            w = slope * t
    high, low = split(r)
    tail = dot(halves(vector), high) + dot(halves(vector), low)
    wmean = (z * vector + (tail[:8] + tail[8:])) * (root * root * (1.0 / (lines - 1)))
    trans = (r + z * ident) * root
    weights = (trans + wmean[:1]).astype(jnp.bfloat16)
    colsum = jnp.sum(weights.astype(jnp.float32), axis=1, keepdims=True)
    for pair in range(0, fields, 2):
        field = jnp.concatenate([rows(pair), rows(pair + 1)], axis=1)
        mean = jnp.sum(field, axis=0, keepdims=True) * (1.0 / lines)
        mixed = dot(weights, field.astype(jnp.bfloat16)) + mean * (1.0 - colsum)
        mixed = jnp.where(live, mixed, field)
        for i in range(2):
            part = mixed[:, i * obs : (i + 1) * obs].reshape(ranks, members, obs)
            out_ref[:, pair + i] = part.astype(jnp.bfloat16)


def edges_kernel(tail_ref, head_ref, tail_out_ref, head_out_ref):
    tail_out_ref[...] = tail_ref[...]
    head_out_ref[...] = head_ref[...]


def pack_kernel(
    me_ref, table_ref, forecast_ref, anomalies_ref, loc_ref, misfit_ref,
    out_ref, chosen_ref, marks_ref, side_ref, blocks_ref, line_ref
):
    count, obs = misfit_ref.shape
    used, slots = table_ref.shape[0] - 1, table_ref.shape[1]
    for field in range(forecast_ref.shape[1]):
        out_ref[:, field] = jnp.swapaxes(forecast_ref[:, field], 0, 1)
    blocks_ref[...] = jnp.swapaxes(anomalies_ref[...], 0, 1)
    tile = marks_ref.shape[2:]
    table = table_ref[...]
    for slot in range(slots):
        for h in range(used):
            index = table[h, slot]
            chosen_ref[slot, h] = blocks_ref[jnp.clip(index - HW, 0, count - 1)]
            marks_ref[slot, h] = jnp.full(tile, index, jnp.int32).astype(marks_ref.dtype)
    me = me_ref[0]
    dead = me >= table[used, 0]
    lane = lax.broadcasted_iota(jnp.int32, table.shape, 1)
    mine = jnp.sum(jnp.where(lane == me, table, 0), axis=1, keepdims=True)
    line_ref[...] = misfit_ref[...].astype(jnp.float32)
    loc = loc_ref[me]
    side_ref[...] = jnp.full(side_ref.shape, jnp.where(dead, 0.0, 1.0), jnp.float32)
    for h in range(used):
        at = slice(h * obs, (h + 1) * obs)
        index = mine[h, 0]
        side_ref[0:1, at] = loc[h : h + 1]
        side_ref[1:2, at] = line_ref[pl.ds(jnp.clip(index - HW, 0, count - 1), 1)]
        side_ref[3:4, at] = jnp.full((1, obs), index, jnp.int32).astype(jnp.float32)


def choose_kernel(
    fields, count, packed_ref, chosen_ref, marks_ref, rows_ref, before_ref, after_ref, out_ref, side_ref
):
    slots, used, members, obs = chosen_ref.shape
    out_ref[:, :fields] = packed_ref[...]
    ends = []
    for ref, first in ((before_ref, 0), (after_ref, HW + count)):
        edge = jnp.swapaxes(ref[:members], 0, 1)
        line = ref[members].astype(jnp.float32)
        ends += [(first + i, edge[i], line[i : i + 1]) for i in range(HW)]
    for h in range(used):
        marks, chosen = marks_ref[:, h], chosen_ref[:, h]
        for index, block, _ in ends:
            chosen = jnp.where(marks == jnp.bfloat16(index), block[None], chosen)
        out_ref[:, fields + h] = chosen
    side_ref[...] = rows_ref[...]
    marks, innov = rows_ref[3:4], rows_ref[1:2]
    for index, _, line in ends:
        innov = jnp.where(marks == index, jnp.concatenate([line] * used, axis=1), innov)
    side_ref[1:2] = innov


def shards(forecast, anomalies, misfit, precision, table, tally):
    members, slots, fields, cells = forecast.shape
    used = table.shape[1]
    count, obs = misfit.shape
    table = jnp.transpose(table)
    ranks = lax.axis_size("member")
    regions = lax.axis_size("region")
    stacked = jnp.concatenate([anomalies, misfit[None]], axis=0)
    up = [(i, (i + 1) % regions) for i in range(regions)]
    edge = jax.ShapeDtypeStruct((members + 1, HW, obs), anomalies.dtype)
    tail, head = pl.pallas_call(
        edges_kernel,
        out_shape=(edge, edge),
        in_specs=[VMEM, VMEM],
        out_specs=(VMEM, VMEM),
        compiler_params=PARAMS,
        cost_estimate=pl.CostEstimate(flops=8 * 10**9, bytes_accessed=10**6, transcendentals=0),
        name="edges",
    )(stacked[:, count - HW :], stacked[:, :HW])
    before = lax.ppermute(tail, "region", up)
    after = lax.ppermute(head, "region", [(j, i) for i, j in up])
    order = [(19 - i) % ranks for i in range(ranks)]
    me = lax.axis_index("member").reshape(1)
    me = (19 - me + ranks) % ranks
    table = jnp.concatenate([table, jnp.broadcast_to(tally[None], (1, slots))], axis=0)
    blocks = jax.ShapeDtypeStruct((slots, used, members, obs), anomalies.dtype)
    rows = jax.ShapeDtypeStruct((8, used * obs), jnp.float32)
    packed, chosen, marks, side = pl.pallas_call(
        pack_kernel,
        out_shape=(
            jax.ShapeDtypeStruct((slots, fields, members, cells), forecast.dtype),
            blocks,
            blocks,
            rows,
        ),
        in_specs=[SMEM] + [VMEM] * 5,
        out_specs=(VMEM,) * 4,
        scratch_shapes=[
            pltpu.VMEM((count, members, obs), anomalies.dtype),
            pltpu.VMEM((count, obs), jnp.float32),
        ],
        compiler_params=PARAMS,
        name="pack",
    )(me, table, jnp.transpose(forecast, (0, 2, 1, 3)), anomalies, precision, misfit)
    outgoing, side = pl.pallas_call(
        functools.partial(choose_kernel, fields, count),
        out_shape=(
            jax.ShapeDtypeStruct((slots, fields + used, members, cells), packed.dtype),
            rows,
        ),
        in_specs=[VMEM] * 6,
        out_specs=(VMEM, VMEM),
        compiler_params=PARAMS,
        name="choose",
    )(packed, chosen, marks, side, before, after)
    incoming = lax.all_to_all(outgoing, "member", 0, 0, tiled=True, axis_index_groups=[order])
    back = pl.pallas_call(
        functools.partial(analyse_kernel, fields),
        out_shape=jax.ShapeDtypeStruct((ranks, fields, members, cells), forecast.dtype),
        in_specs=[VMEM, VMEM],
        out_specs=VMEM,
        compiler_params=PARAMS,
        name="analyse",
    )(incoming, side)
    back = lax.all_to_all(back, "member", 0, 0, tiled=True, axis_index_groups=[order])
    return jnp.transpose(back, (2, 0, 1, 3))


def solution(mesh):
    return jax.shard_map(
        shards,
        mesh=mesh,
        in_specs=(
            P("member", "region", None, None),
            P("member", "region", None),
            P("region", None),
            P("region", None, None),
            P("region", None),
            P("region"),
        ),
        out_specs=P("member", "region", None, None),
        check_vma=False,
    )
```
